256 devices in a mesh: dom: 32 (over z, y), sub: 8 (over x, core).
Axes of the slice: x: 4, y: 4, z: 8, core: 2. Of those that a mesh axis runs over, the one named last changes fastest.
Arguments:
- node: bfloat16 [32, 8, 512, 128], P('dom', 'sub'), may hold values from -6 to 6
- edges: bfloat16 [32, 8, 2048, 128], P('dom', 'sub'), may hold values from -6 to 6
- edge_src: int32 [32, 8, 2048], P('dom', 'sub'), may hold values from 0 to 703, as said below
- edge_dst: int32 [32, 8, 2048], P('dom', 'sub'), may hold values from 0 to 511, as said below
- edge_count: int32 [32, 8], P('dom', 'sub'), may hold values from 768 to 2048, as said below
- intra_idx: int32 [32, 8, 8, 8], P('dom', 'sub'), may hold values from 0 to 511, as said below
- bound_idx: int32 [32, 8, 2, 16], P('dom', 'sub'), may hold values from 0 to 511, as said below
- cross_pick: int32 [8, 2, 8, 8], P('sub'), may hold values from 0 to 15, as said below
- match_send: int32 [32, 8, 8, 16], P('dom', 'sub'), may hold values from 0 to 511, as said below
- pool_first: int32 [32, 8, 256], P('dom', 'sub'), may hold values from 0 to 511, as said below
- pool_second: int32 [32, 8, 256], P('dom', 'sub'), may hold values from 0 to 639, as said below
- edge_w1: bfloat16 [384, 128], replicated, may hold values from -0.3125 to 0.3125
- edge_b1: float32 [128], replicated, may hold values from -3 to 3
- edge_w2: bfloat16 [128, 128], replicated, may hold values from -0.5 to 0.5
- edge_gain: float32 [128], replicated, may hold values from 0.25 to 1.75
- node_w1: bfloat16 [256, 128], replicated, may hold values from -0.375 to 0.375
- node_b1: float32 [128], replicated, may hold values from -3 to 3
- node_w2: bfloat16 [128, 128], replicated, may hold values from -0.5 to 0.5
- node_gain: float32 [128], replicated, may hold values from 0.25 to 1.75
- edge_cot: bfloat16 [32, 8, 2048, 128], P('dom', 'sub'), may hold values from -8 to 8
- coarse_cot: bfloat16 [32, 8, 256, 128], P('dom', 'sub'), may hold values from -8 to 8
Outputs:
- new_edges: bfloat16 [32, 8, 2048, 128], P('dom', 'sub')
- coarse: bfloat16 [32, 8, 256, 128], P('dom', 'sub')
- d_node: float32 [32, 8, 512, 128], P('dom', 'sub')
- d_edges: bfloat16 [32, 8, 2048, 128], P('dom', 'sub')
- grad_edge_w1: float32 [384, 128], replicated
- grad_edge_b1: float32 [128], replicated
- grad_edge_w2: float32 [128, 128], replicated
- grad_edge_gain: float32 [128], replicated
- grad_node_w1: float32 [256, 128], replicated
- grad_node_b1: float32 [128], replicated
- grad_node_w2: float32 [128, 128], replicated
- grad_node_gain: float32 [128], replicated
The draws below stay inside these ranges and needn't reach their ends.
Inputs may be any that keep to these rules, and one draw needn't show every extreme that they name: `edge_src`: edges of slab 0 never refer to kind 1 row and edges of the last slab never to kind 2 rows. `edge_dst`: Non-decreasing along each device's slots. `edge_count`: A multiple of 128; some device in every draw has all 2048 slots live. `intra_idx`: distinct within each list. `bound_idx`: all 32 cells of a device are distinct. `cross_pick`: for each s and k, every face position appears exactly 4 times over the 8 x 8 entries; the same on every slab. `match_send`: together with pool_first and pool_second every cell of every device belongs to exactly one coarse cell. `pool_first`: never a cell listed in the device's match_send. `pool_second`: values of 512 or more name received rows, each exactly once.
All inputs are finite; a program needn't handle non-finite values.
Results may differ from the reference program's by a relative error of at most 0.0062.
Values may be sent and summed in bfloat16 or wider, within the bound.
No kernel may reach another device: no remote copies, remote signals or barrier semaphores. Data moves between devices by JAX's collectives and lax.ppermute only.
A program may use at most 64 MiB of HBM per device.

```python
import math
import jax
import jax.numpy as jnp
from jax import lax

H = 128
CELL_DEV = 512
FAN = 4
EDGE_DEV = 2048
HALO = 8
BOUND = 16
MATCH = 16
COARSE = 256
ALL_EDGES = 524288
N_DOM = 32
N_SUB = 8


def slab_ramp(rank_count):
    ramp = 0.5 + jnp.arange(N_DOM, dtype=jnp.float32) / (N_DOM - 1)
    return ramp.reshape((N_DOM,) + (1,) * (rank_count - 1))


def matching(key):
    key_list = jax.random.split(key, N_DOM * N_SUB)

    def one_device(device_key):
        ordering = jax.random.permutation(jax.random.fold_in(device_key, 1), CELL_DEV)
        shuffle = jax.random.permutation(jax.random.fold_in(device_key, 2), COARSE)
        spread = N_SUB * MATCH
        kept_cells = ordering[spread:]
        positions = jnp.arange(COARSE)
        tail_index = jnp.clip(positions - spread + COARSE, 0, CELL_DEV - spread - 1)
        second_ids = jnp.where(positions < spread, CELL_DEV + positions, jnp.take(kept_cells, tail_index))
        first_ids = kept_cells[:COARSE]
        return (ordering[:spread].reshape(N_SUB, MATCH), jnp.take(first_ids, shuffle), jnp.take(second_ids, shuffle))
    sent_ids, first_ids, second_ids = jax.vmap(one_device)(key_list)
    return (sent_ids.reshape(N_DOM, N_SUB, N_SUB, MATCH).astype(jnp.int32), first_ids.reshape(N_DOM, N_SUB, COARSE).astype(jnp.int32), second_ids.reshape(N_DOM, N_SUB, COARSE).astype(jnp.int32))


def draw_match_send(key, part):
    return matching(key)[0]


def draw_pool_first(key, part):
    return matching(key)[1]


def draw_pool_second(key, part):
    return matching(key)[2]


def draw_edge_src(key, part):
    key = jax.random.fold_in(key, 1)
    key_one, key_two, key_three, key_four = jax.random.split(key, 4)
    dims_all = (N_DOM, N_SUB, EDGE_DEV)
    local_ids = jax.random.randint(key_one, dims_all, 0, CELL_DEV)
    kind_ids = jax.random.randint(key_two, dims_all, 0, 3)
    slab_index = jnp.arange(N_DOM)[:, None, None]
    kind_ids = jnp.where((slab_index == 0) & (kind_ids == 1), 0, kind_ids)
    kind_ids = jnp.where((slab_index == N_DOM - 1) & (kind_ids == 2), 0, kind_ids)
    slot_ids = jax.random.randint(key_three, dims_all, 0, N_SUB * HALO)
    remote = CELL_DEV + kind_ids * (N_SUB * HALO) + slot_ids
    pick_halo = jax.random.randint(key_four, dims_all, 0, 10) < 3
    sources = jnp.where(pick_halo, remote, local_ids)
    sources = sources.at[0, 0, 0].set(CELL_DEV + 3 * N_SUB * HALO - 1)
    return sources.astype(jnp.int32)


def draw_edge_dst(key, part):
    key = jax.random.fold_in(key, 2)
    targets = jax.random.randint(key, (N_DOM, N_SUB, EDGE_DEV), 0, CELL_DEV)
    return jnp.sort(targets, axis=-1).astype(jnp.int32)


def draw_edge_count(key, part):
    key = jax.random.fold_in(key, 3)
    key_one, key_two = jax.random.split(key)
    blocks = EDGE_DEV // 128
    least_blocks = max(1, 3 * blocks // 8)
    counts = jax.random.randint(key_one, (N_DOM * N_SUB,), least_blocks, blocks + 1) * 128
    full_device = jax.random.randint(key_two, (), 0, N_DOM * N_SUB)
    counts = jnp.where(jnp.arange(N_DOM * N_SUB) == full_device, EDGE_DEV, counts)
    return counts.reshape(N_DOM, N_SUB).astype(jnp.int32)


def draw_intra_idx(key, part):
    key = jax.random.fold_in(key, 4)
    key_list = jax.random.split(key, N_DOM * N_SUB * N_SUB)
    row_ids = jax.vmap(lambda each_key: jax.random.permutation(each_key, CELL_DEV)[:HALO])(key_list)
    return row_ids.reshape(N_DOM, N_SUB, N_SUB, HALO).astype(jnp.int32)


def draw_bound_idx(key, part):
    key = jax.random.fold_in(key, 5)
    key_list = jax.random.split(key, N_DOM * N_SUB)
    row_ids = jax.vmap(lambda each_key: jax.random.permutation(each_key, CELL_DEV)[:2 * BOUND])(key_list)
    return row_ids.reshape(N_DOM, N_SUB, 2, BOUND).astype(jnp.int32)


def draw_cross_pick(key, part):
    key = jax.random.fold_in(key, 6)
    key_list = jax.random.split(key, N_SUB * 2)
    repeated = jnp.tile(jnp.arange(BOUND), FAN)
    row_ids = jax.vmap(lambda each_key: jax.random.permutation(each_key, repeated))(key_list)
    return row_ids.reshape(N_SUB, 2, N_SUB, HALO).astype(jnp.int32)


def draw_edge_cot(key, part):
    key = jax.random.fold_in(key, 11)
    key_one = jax.random.fold_in(key, 0)
    dims_all = (N_DOM, N_SUB, EDGE_DEV, H)
    base_draw = jnp.clip(jax.random.normal(key_one, dims_all, jnp.float32), -4.0, 4.0)
    return jnp.clip(base_draw * slab_ramp(4), -8.0, 8.0).astype(jnp.bfloat16)


def draw_coarse_cot(key, part):
    key = jax.random.fold_in(key, 13)
    key_one = jax.random.fold_in(key, 0)
    dims_all = (N_DOM, N_SUB, COARSE, H)
    base_draw = jnp.clip(jax.random.normal(key_one, dims_all, jnp.float32), -4.0, 4.0)
    return jnp.clip(base_draw * slab_ramp(4), -8.0, 8.0).astype(jnp.bfloat16)


def levels(own_key, extent, shards, low, high):
    def one(position, blocks):
        heights = jax.random.uniform(jax.random.fold_in(jax.random.fold_in(own_key, 6), position), (blocks,), jnp.float32, low / len(shards), high / len(shards))
        return jnp.repeat(jnp.exp(heights), extent[position] // blocks).reshape((-1,) + (1,) * (len(extent) - position - 1))

    factor_of = one(*shards[0])
    for cut in shards[1:]:
        factor_of = factor_of * one(*cut)
    return factor_of


def bell_draw(stream_key, dims, scale, reach, pieces=(), kind=jnp.bfloat16):
    values = jax.random.normal(stream_key, dims, jnp.float32) * scale
    if len(pieces) > 0:
        values = levels(stream_key, dims, pieces, -0.22, 0.18) * values
    return jnp.clip(values, min=-reach, max=reach).astype(kind)


def setup_inputs(seed: int = 0) -> dict:
    seeds = jax.random.split(jax.random.key(seed), 22)
    return {
        "node": bell_draw(seeds[0], (N_DOM, N_SUB, CELL_DEV, H), 1.0, 6.0, ((0, 32), (1, 8))),
        "edges": bell_draw(seeds[1], (N_DOM, N_SUB, EDGE_DEV, H), 1.0, 6.0, ((0, 32), (1, 8))),
        "edge_src": draw_edge_src(jax.random.fold_in(seeds[21], 71), 0),
        "edge_dst": draw_edge_dst(jax.random.fold_in(seeds[21], 71), 0),
        "edge_count": draw_edge_count(jax.random.fold_in(seeds[21], 71), 0),
        "intra_idx": draw_intra_idx(jax.random.fold_in(seeds[21], 71), 0),
        "bound_idx": draw_bound_idx(jax.random.fold_in(seeds[21], 71), 0),
        "cross_pick": draw_cross_pick(jax.random.fold_in(seeds[21], 71), 0),
        "match_send": draw_match_send(jax.random.fold_in(seeds[21], 71), 0),
        "pool_first": draw_pool_first(jax.random.fold_in(seeds[21], 71), 0),
        "pool_second": draw_pool_second(jax.random.fold_in(seeds[21], 71), 0),
        "edge_w1": bell_draw(seeds[11], (3 * H, H), (3 * H) ** -0.5, 0.3125),
        "edge_b1": bell_draw(seeds[12], (H,), 0.5, 3.0, (), jnp.float32),
        "edge_w2": bell_draw(seeds[13], (H, H), H ** -0.5, 0.5),
        "edge_gain": jnp.clip(1.0 + 0.15 * jax.random.normal(seeds[14], (H,), jnp.float32), 0.25, 1.75),
        "node_w1": bell_draw(seeds[15], (2 * H, H), (2 * H) ** -0.5, 0.375),
        "node_b1": bell_draw(seeds[16], (H,), 0.5, 3.0, (), jnp.float32),
        "node_w2": bell_draw(seeds[17], (H, H), H ** -0.5, 0.5),
        "node_gain": jnp.clip(1.0 + 0.15 * jax.random.normal(seeds[18], (H,), jnp.float32), 0.25, 1.75),
        "edge_cot": draw_edge_cot(jax.random.fold_in(seeds[21], 71), 0),
        "coarse_cot": draw_coarse_cot(jax.random.fold_in(seeds[21], 71), 0),
    }


NORM_EPSILON = 1e-05

def layer_norm(values, gain_vec):
    average = lax.optimization_barrier(jnp.mean(values, axis=-1, keepdims=True))
    centred = values - average
    variance = lax.optimization_barrier(jnp.mean(centred * centred, axis=-1, keepdims=True))
    inv_std = lax.rsqrt(variance + NORM_EPSILON)
    normed = centred * inv_std
    return (normed * gain_vec, normed, inv_std)

def norm_backward(upstream, normed, inv_std, gain_vec):
    scaled = upstream * gain_vec
    inner = scaled - lax.optimization_barrier(jnp.mean(scaled, axis=-1, keepdims=True)) - normed * lax.optimization_barrier(jnp.mean(scaled * normed, axis=-1, keepdims=True))
    return (inner * inv_std, lax.optimization_barrier(jnp.sum(upstream * normed, axis=0)))

def mlp_forward(inputs, first_w, first_b, second_w, gain_vec):
    pre_act = jnp.dot(inputs, first_w, preferred_element_type=jnp.float32) + first_b
    activation = jax.nn.silu(pre_act).astype(jnp.bfloat16)
    projected = jnp.dot(activation, second_w, preferred_element_type=jnp.float32)
    result, normed, inv_std = layer_norm(projected, gain_vec)
    return (result, (pre_act, activation, normed, inv_std))

def mlp_backward(upstream, inputs, saved_vals, first_w, second_w, gain_vec):
    pre_act, activation, normed, inv_std = saved_vals
    d_projected, d_gain = norm_backward(upstream, normed, inv_std, gain_vec)
    d_proj_half = d_projected.astype(jnp.bfloat16)
    d_second = jnp.dot(activation.T, d_proj_half, preferred_element_type=jnp.float32)
    d_activation = jnp.dot(d_proj_half, second_w.T, preferred_element_type=jnp.float32)
    sigmoid_pre = jax.nn.sigmoid(pre_act)
    d_pre = d_activation * sigmoid_pre * (1.0 + pre_act * (1.0 - sigmoid_pre))
    d_pre_half = d_pre.astype(jnp.bfloat16)
    d_first = jnp.dot(inputs.T, d_pre_half, preferred_element_type=jnp.float32)
    d_inputs = jnp.dot(d_pre_half, first_w.T, preferred_element_type=jnp.float32)
    return (d_inputs, (d_first, lax.optimization_barrier(jnp.sum(d_pre, axis=0)), d_second, d_gain))

def layer_forward(node_here, row_table, edge_here, source_ids, target_ids, live_count, weights):
    edge_w1, edge_b1, edge_w2, edge_gain, node_w1, node_b1, node_w2, node_gain = weights
    cell_count = node_here.shape[0]
    live_mask = (jnp.arange(edge_here.shape[0]) < live_count)[:, None]
    edge_inputs = jnp.concatenate([edge_here, jnp.take(row_table, source_ids, axis=0), jnp.take(node_here, target_ids, axis=0)], axis=1)
    message, edge_saved = mlp_forward(edge_inputs, edge_w1, edge_b1, edge_w2, edge_gain)
    message = jnp.where(live_mask, message, 0.0)
    new_edge = jnp.where(live_mask, edge_here.astype(jnp.float32) + message, 0.0).astype(jnp.bfloat16)
    aggregate = jax.ops.segment_sum(message, target_ids, num_segments=cell_count, indices_are_sorted=True).astype(jnp.bfloat16)
    node_inputs = jnp.concatenate([node_here, aggregate], axis=1)
    update, node_saved = mlp_forward(node_inputs, node_w1, node_b1, node_w2, node_gain)
    fresh = (node_here.astype(jnp.float32) + update).astype(jnp.bfloat16)
    return (new_edge, fresh, (live_mask, edge_inputs, edge_saved, node_inputs, node_saved))

def layer_backward(saved, d_fresh, edge_cot_here, target_ids, source_ids, table_rows, weights):
    edge_w1, edge_b1, edge_w2, edge_gain, node_w1, node_b1, node_w2, node_gain = weights
    live_mask, edge_inputs, edge_saved, node_inputs, node_saved = saved
    cell_count, feature = d_fresh.shape
    d_node_in, node_grads = mlp_backward(d_fresh, node_inputs, node_saved, node_w1, node_w2, node_gain)
    cot_here = jnp.where(live_mask, edge_cot_here.astype(jnp.float32), 0.0)
    d_message = jnp.where(live_mask, cot_here + jnp.take(d_node_in[:, feature:], target_ids, axis=0), 0.0)
    d_edge_in, edge_grads = mlp_backward(d_message, edge_inputs, edge_saved, edge_w1, edge_w2, edge_gain)
    d_edge = (cot_here + d_edge_in[:, :feature]).astype(jnp.bfloat16)
    d_node = d_fresh + d_node_in[:, :feature] + jax.ops.segment_sum(d_edge_in[:, 2 * feature:], target_ids, num_segments=cell_count, indices_are_sorted=True)
    d_table = jax.ops.segment_sum(d_edge_in[:, feature:2 * feature], source_ids, num_segments=table_rows)
    d_node = d_node + d_table[:cell_count]
    return (d_edge, d_node, d_table[cell_count:], edge_grads + node_grads)

def take_each(row_sets, id_sets):
    return jax.vmap(jax.vmap(lambda rows, ids: jnp.take(rows, ids, axis=0)))(row_sets, id_sets)

def add_each(base_sets, id_sets, value_sets):
    return jax.vmap(jax.vmap(lambda base, ids, values: base.at[ids].add(values)))(base_sets, id_sets, value_sets)

def face_lists(face_ids, pick_ids):
    return jnp.stack([jnp.take(face_ids[0], pick_ids[0]), jnp.take(face_ids[1], pick_ids[1])])

def reference(node, edges, edge_src, edge_dst, edge_count, intra_idx, bound_idx, cross_pick, match_send, pool_first, pool_second, edge_w1, edge_b1, edge_w2, edge_gain, node_w1, node_b1, node_w2, node_gain, edge_cot, coarse_cot):
    weights = (edge_w1, edge_b1, edge_w2, edge_gain, node_w1, node_b1, node_w2, node_gain)
    slabs, peers, cell_count, feature = node.shape
    halo_rows = intra_idx.shape[-1]
    intra_rows = take_each(node, intra_idx.reshape(slabs, peers, -1)).reshape(slabs, peers, peers, halo_rows, feature)
    face_cells = jax.vmap(lambda faces_here: jax.vmap(face_lists)(faces_here, cross_pick))(bound_idx)
    face_rows = take_each(node, face_cells.reshape(slabs, peers, -1)).reshape(slabs, peers, 2, peers, halo_rows, feature)
    empty_rows = jnp.zeros_like(face_rows[:1, :, 0])
    from_below = jnp.concatenate([empty_rows, face_rows[:-1, :, 1]], axis=0)
    from_above = jnp.concatenate([face_rows[1:, :, 0], empty_rows], axis=0)
    stacked = jnp.stack([intra_rows, from_below, from_above], axis=2)
    received = jnp.transpose(stacked, (0, 3, 2, 1, 4, 5)).reshape(slabs, peers, 3 * peers * halo_rows, feature)
    row_table = jnp.concatenate([node, received], axis=2)
    table_rows = row_table.shape[2]
    devices = slabs * peers

    def flatten(array):
        return array.reshape((devices,) + array.shape[2:])
    forward_in = (flatten(node), flatten(row_table), flatten(edges), flatten(edge_src), flatten(edge_dst), flatten(edge_count))

    def run_forward(item):
        new_edge, fresh_here, unused = layer_forward(item[0], item[1], item[2], item[3], item[4], item[5], weights)
        return (new_edge, fresh_here)
    new_edges, fresh = lax.map(run_forward, forward_in)
    fresh = fresh.reshape(slabs, peers, cell_count, feature)
    match_ids = match_send.reshape(slabs, peers, -1)
    match_rows = take_each(fresh, match_ids).reshape(slabs, peers, peers, -1, feature)
    partners = jnp.transpose(match_rows, (0, 2, 1, 3, 4)).reshape(slabs, peers, -1, feature)
    pool_table = jnp.concatenate([fresh, partners], axis=2)
    coarse = (0.5 * (take_each(fresh, pool_first).astype(jnp.float32) + take_each(pool_table, pool_second).astype(jnp.float32))).astype(jnp.bfloat16)
    half_grad = 0.5 * coarse_cot.astype(jnp.float32)
    d_pool = add_each(jnp.zeros(pool_table.shape, jnp.float32), pool_second, half_grad)
    d_fresh = add_each(jnp.zeros(fresh.shape, jnp.float32), pool_first, half_grad) + d_pool[:, :, :cell_count]
    returned = jnp.transpose(d_pool[:, :, cell_count:].reshape(slabs, peers, peers, -1, feature), (0, 2, 1, 3, 4)).reshape(slabs, peers, -1, feature)
    d_fresh = add_each(d_fresh, match_ids, returned)
    backward_in = forward_in + (flatten(d_fresh), flatten(edge_cot))

    def run_backward(item):
        node_here, table_here, edge_here, source_ids, target_ids, live_count, d_fresh_here, cot_here = item
        unused_edge, unused_fresh, saved = layer_forward(node_here, table_here, edge_here, source_ids, target_ids, live_count, weights)
        return layer_backward(saved, d_fresh_here, cot_here, target_ids, source_ids, table_rows, weights)
    d_edges, d_node, d_halo, grads = lax.map(run_backward, backward_in)
    d_halo = d_halo.reshape(slabs, peers, 3, peers, halo_rows, feature)
    d_sent = jnp.transpose(d_halo, (0, 3, 2, 1, 4, 5))
    d_node = d_node.reshape(slabs, peers, cell_count, feature)
    d_node = add_each(d_node, intra_idx.reshape(slabs, peers, -1), d_sent[:, :, 0].reshape(slabs, peers, -1, feature))
    zero_grad = jnp.zeros_like(d_sent[:1, :, 1])
    d_upper = jnp.concatenate([d_sent[1:, :, 1], zero_grad], axis=0)
    d_lower = jnp.concatenate([zero_grad, d_sent[:-1, :, 2]], axis=0)
    d_faces = jnp.stack([d_lower, d_upper], axis=2).reshape(slabs, peers, -1, feature)
    d_node = add_each(d_node, face_cells.reshape(slabs, peers, -1), d_faces)
    grad_scale = 1.0 / math.sqrt(ALL_EDGES)
    return (new_edges.reshape(edges.shape), coarse, d_node, d_edges.reshape(edges.shape), lax.optimization_barrier(jnp.sum(grads[0], axis=0)) * grad_scale, lax.optimization_barrier(jnp.sum(grads[1], axis=0)) * grad_scale, lax.optimization_barrier(jnp.sum(grads[2], axis=0)) * grad_scale, lax.optimization_barrier(jnp.sum(grads[3], axis=0)) * grad_scale, lax.optimization_barrier(jnp.sum(grads[4], axis=0)) * grad_scale, lax.optimization_barrier(jnp.sum(grads[5], axis=0)) * grad_scale, lax.optimization_barrier(jnp.sum(grads[6], axis=0)) * grad_scale, lax.optimization_barrier(jnp.sum(grads[7], axis=0)) * grad_scale)
```

```python
import functools
import math

import jax
import jax.numpy as jnp
from jax import lax
from jax.experimental import pallas as pl
from jax.experimental.pallas import tpu as pltpu
from jax.sharding import Mesh
from jax.sharding import PartitionSpec as P

NORM_EPSILON = 1e-05
F32 = jnp.float32
BF16 = jnp.bfloat16
TILE = 256
VMEM_LIMIT = 56 * 1024 * 1024

ROWS_ONE = 48
ROWS_TWO = 176
GRAD_ROWS = 128


def mm(a, b):
    return lax.dot_general(a, b, (((1,), (0,)), ((), ())), preferred_element_type=F32)


def mm_nt(a, b):
    return lax.dot_general(a, b, (((1,), (1,)), ((), ())), preferred_element_type=F32)


def mm_tn(a, b):
    return lax.dot_general(a, b, (((0,), (0,)), ((), ())), preferred_element_type=F32)


def iota(shape, dim):
    return lax.broadcasted_iota(jnp.int32, shape, dim)


def onehot(mask):
    return jnp.where(mask, 1.0, 0.0).astype(BF16)


def two_parts(x):
    high = x.astype(BF16)
    low = (x - high.astype(F32)).astype(BF16)
    return high, low


def column_of(ids):
    a, b = ids.shape
    spread = jnp.broadcast_to(ids[:, None, :], (a, b, b))
    keep = iota((a, b, b), 1) == iota((a, b, b), 2)
    return jnp.sum(jnp.where(keep, spread, 0), axis=2, keepdims=True).reshape(a * b, 1)


def face_column(face_row, pick):
    spot = column_of(pick)
    shape = (spot.shape[0], face_row.shape[1])
    keep = spot == iota(shape, 1)
    return jnp.sum(jnp.where(keep, jnp.broadcast_to(face_row, shape), 0), axis=1, keepdims=True)


def onehot_rows(column, width):
    return onehot(column == iota((column.shape[0], width), 1))


def face_kernel(node_ref, bound_ref, pick_ref, down_ref, up_ref):
    node = node_ref[...]
    for k, out_ref in ((0, down_ref), (1, up_ref)):
        column = face_column(bound_ref[k : k + 1, :], pick_ref[k])
        out_ref[...] = mm(onehot_rows(column, node.shape[0]), node).astype(BF16)


def send_kernel(node_ref, intra_ref, second_ref, coarse_cot_ref, below_ref, above_ref, out_ref):
    node = node_ref[...]
    cells, feature = node.shape
    peers, halo = intra_ref.shape
    coarse = coarse_cot_ref.shape[0]
    intra = mm(onehot_rows(column_of(intra_ref[...]), cells), node)
    half = 0.5 * coarse_cot_ref[...].astype(F32)
    pool_rows = 16 * peers
    pool = mm(onehot(second_ref[...] - cells == iota((pool_rows, coarse), 0)), half.astype(BF16))
    parts = [
        intra.reshape(peers, halo, feature),
        below_ref[...].astype(F32).reshape(peers, halo, feature),
        above_ref[...].astype(F32).reshape(peers, halo, feature),
        jnp.zeros((peers, halo, feature), F32),
        pool.reshape(peers, 16, feature),
    ]
    out_ref[...] = jnp.concatenate(parts, axis=1).astype(BF16)


def silu_parts(pre):
    sig = 0.5 * jnp.tanh(0.5 * pre) + 0.5
    act = (pre * sig).astype(BF16)
    slope = sig * (1.0 + pre * (1.0 - sig))
    return act, slope


def norm_forward(out):
    centred = out - jnp.mean(out, axis=1, keepdims=True)
    inv = lax.rsqrt(jnp.mean(centred * centred, axis=1, keepdims=True) + NORM_EPSILON)
    return centred * inv, inv


def norm_backward(u, normed, inv, gain):
    scaled = u * gain
    inner = (
        scaled
        - jnp.mean(scaled, axis=1, keepdims=True)
        - normed * jnp.mean(scaled * normed, axis=1, keepdims=True)
    )
    return inner * inv


def fold_rows(x):
    rows, feature = x.shape
    return jnp.sum(x.reshape(rows // 8, 8, feature), axis=0)


def main_kernel(
    count_ref, src_ref, dst_ref, node_ref, recv_ref, edges_ref, cot_ref, coarse_cot_ref,
    first_ref, second_ref, match_ref, ew1_ref, eb1_ref, ew2_ref, eg_ref,
    nw1_ref, nb1_ref, nw2_ref, ng_ref,
    new_edges_ref, d_edges_ref, d_node_ref, fresh_ref, send_ref,
    table_ref, t2_ref, ohd_ref, oht_ref, agg_ref, act_ref, slope_ref, normed_ref, inv_ref,
    dagg_ref, s_ref, dw1_ref, dw2_ref, db1_ref, dg_ref, grads_ref,
):
    cells, feature = node_ref.shape
    slots = edges_ref.shape[0]
    peers = recv_ref.shape[0]
    tiles = slots // TILE
    count = count_ref[0, 0]
    node = node_ref[...]
    received = recv_ref[...].astype(F32)
    halo_rows = 3 * 8 * peers
    wide = table_ref.shape[0]
    table_ref[0:cells, :] = node
    halo = jnp.concatenate(
        [received[:, 8 * k : 8 * k + 8, :].reshape(8 * peers, feature) for k in range(3)]
        + [jnp.zeros((wide - cells - halo_rows, feature), F32)],
        axis=0,
    )
    table_ref[cells:wide, :] = halo.astype(BF16)
    ew1_edge = ew1_ref[0:feature, :]
    ew1_src = ew1_ref[feature : 2 * feature, :]
    ew1_dst = ew1_ref[2 * feature : 3 * feature, :]
    high, low = two_parts(mm(table_ref[...], ew1_src))
    t2_ref[0:wide, 0:feature] = high
    t2_ref[0:wide, feature:] = low
    high, low = two_parts(mm(node, ew1_dst) + eb1_ref[...])
    t2_ref[wide:, 0:feature] = high
    t2_ref[wide:, feature:] = low
    agg_ref[...] = jnp.zeros_like(agg_ref)
    ew2 = ew2_ref[...]
    eg = eg_ref[...]

    def live_of(start):
        return iota((TILE, feature), 0) + start < count

    def forward_tile(i, carry):
        start = pl.multiple_of(i * TILE, TILE)
        rows = pl.ds(start, TILE)
        src = src_ref[:, rows]
        dst = dst_ref[:, rows]
        src_col = jnp.broadcast_to(src, (128, TILE)).T
        dst_col = jnp.broadcast_to(dst, (128, TILE)).T
        lane = iota((TILE, 128), 1)
        hot_src = jnp.concatenate(
            [onehot(src_col == lane + 128 * k) for k in range(wide // 128)], axis=1
        )
        hot_dst = jnp.concatenate(
            [onehot(dst_col == lane + 128 * k) for k in range(cells // 128)], axis=1
        )
        ohd_ref[rows, :] = hot_dst
        both = mm(hot_src, t2_ref[0:wide, :]) + mm(hot_dst, t2_ref[wide:, :])
        edges = edges_ref[rows, :]
        pre = both[:, 0:feature] + both[:, feature:] + mm(edges, ew1_edge)
        act, slope = silu_parts(pre)
        act_ref[rows, :] = act
        slope_ref[rows, :] = slope
        normed, inv = norm_forward(mm(act, ew2))
        normed_ref[rows, :] = normed
        inv_ref[rows, :] = inv
        live = live_of(start)
        message = jnp.where(live, normed * eg, 0.0)
        new_edges_ref[rows, :] = jnp.where(live, edges.astype(F32) + message, 0.0).astype(BF16)
        hot = onehot(dst == iota((cells, TILE), 0))
        oht_ref[:, rows] = hot
        agg_ref[...] += mm(hot, jnp.concatenate(two_parts(message), axis=1))
        return carry

    lax.fori_loop(0, tiles, forward_tile, 0)

    aggregate = (agg_ref[:, 0:feature] + agg_ref[:, feature:]).astype(BF16)
    nw1_node = nw1_ref[0:feature, :]
    nw1_agg = nw1_ref[feature:, :]
    pre = mm(node, nw1_node) + mm(aggregate, nw1_agg) + nb1_ref[...]
    act, slope = silu_parts(pre)
    nw2 = nw2_ref[...]
    ng = ng_ref[...]
    normed, inv = norm_forward(mm(act, nw2))
    fresh = (node.astype(F32) + normed * ng).astype(BF16)
    fresh_ref[...] = fresh

    coarse = coarse_cot_ref.shape[0]
    half = (0.5 * coarse_cot_ref[...].astype(F32)).astype(BF16)
    cell_row = iota((cells, coarse), 0)
    pooled = onehot((first_ref[...] == cell_row) | (second_ref[...] == cell_row))
    returned = recv_ref[:, ROWS_ONE - 16 : ROWS_ONE, :].reshape(16 * peers, feature)
    hot_match = onehot_rows(column_of(match_ref[...]), cells)
    d_fresh = mm(pooled, half) + mm_tn(hot_match, returned)
    match_rows = mm(hot_match, fresh)

    d_out = norm_backward(d_fresh, normed, inv, ng)
    grads_ref[899:900, :] = jnp.sum(d_fresh * normed, axis=0, keepdims=True)
    d_out_half = d_out.astype(BF16)
    grads_ref[768:896, :] = mm_tn(act, d_out_half)
    d_pre = mm_nt(d_out_half, nw2) * slope
    grads_ref[898:899, :] = jnp.sum(d_pre, axis=0, keepdims=True)
    d_pre_half = d_pre.astype(BF16)
    grads_ref[512:640, :] = mm_tn(node, d_pre_half)
    grads_ref[640:768, :] = mm_tn(aggregate, d_pre_half)
    d_node_ref[...] = d_fresh + mm_nt(d_pre_half, nw1_node)
    high, low = two_parts(mm_nt(d_pre_half, nw1_agg))
    dagg_ref[:, 0:feature] = high
    dagg_ref[:, feature:] = low

    s_ref[...] = jnp.zeros_like(s_ref)
    dw1_ref[...] = jnp.zeros_like(dw1_ref)
    dw2_ref[...] = jnp.zeros_like(dw2_ref)
    db1_ref[...] = jnp.zeros_like(db1_ref)
    dg_ref[...] = jnp.zeros_like(dg_ref)

    def backward_tile(i, carry):
        start = pl.multiple_of(i * TILE, TILE)
        rows = pl.ds(start, TILE)
        both = mm(ohd_ref[rows, :], dagg_ref[...])
        live = live_of(start)
        cot = jnp.where(live, cot_ref[rows, :].astype(F32), 0.0)
        u = jnp.where(live, cot + (both[:, 0:feature] + both[:, feature:]), 0.0)
        normed = normed_ref[rows, :]
        d_out_half = norm_backward(u, normed, inv_ref[rows, :], eg).astype(BF16)
        dg_ref[...] += fold_rows(u * normed)
        dw2_ref[...] += mm_tn(act_ref[rows, :], d_out_half)
        d_pre = mm_nt(d_out_half, ew2) * slope_ref[rows, :]
        db1_ref[...] += fold_rows(d_pre)
        d_pre_half = d_pre.astype(BF16)
        d_edges_ref[rows, :] = (cot + mm_nt(d_pre_half, ew1_edge)).astype(BF16)
        dw1_ref[...] += mm_tn(edges_ref[rows, :], d_pre_half)
        hot = onehot(src_ref[:, rows] == iota((wide, TILE), 0))
        s_ref[0:wide, :] += mm(hot, d_pre_half)
        s_ref[wide:, :] += mm(oht_ref[:, rows], d_pre_half)
        return carry

    lax.fori_loop(0, tiles, backward_tile, 0)

    grads_ref[0:128, :] = dw1_ref[...]
    grads_ref[384:512, :] = dw2_ref[...]
    grads_ref[896:897, :] = jnp.sum(db1_ref[...], axis=0, keepdims=True)
    grads_ref[897:898, :] = jnp.sum(dg_ref[...], axis=0, keepdims=True)
    grads_ref[900:, :] = jnp.zeros_like(grads_ref[900:, :])
    high, low = two_parts(s_ref[0:wide, :])
    table = table_ref[...]
    grads_ref[128:256, :] = mm_tn(table, high) + mm_tn(table, low)
    d_table = mm_nt(high, ew1_src) + mm_nt(low, ew1_src)
    high, low = two_parts(s_ref[wide:, :])
    grads_ref[256:384, :] = mm_tn(node, high) + mm_tn(node, low)
    d_node_ref[...] += d_table[0:cells, :] + (mm_nt(high, ew1_dst) + mm_nt(low, ew1_dst))
    kinds = [
        d_table[cells + 8 * peers * k : cells + 8 * peers * (k + 1), :].reshape(peers, 8, feature)
        for k in range(3)
    ]
    parts = kinds + [
        jnp.zeros((peers, 8, feature), F32),
        match_rows.reshape(peers, 16, feature),
        grads_ref[...].reshape(peers, GRAD_ROWS, feature),
    ]
    send_ref[...] = jnp.concatenate(parts, axis=1).astype(BF16)


def split_kernel(recv_ref, down_ref, up_ref, sum_ref):
    peers, _, feature = recv_ref.shape
    head = recv_ref[:, 0:32, :].astype(F32)
    down_ref[...] = head[:, 8:16, :].reshape(8 * peers, feature).astype(BF16)
    up_ref[...] = head[:, 16:24, :].reshape(8 * peers, feature).astype(BF16)
    total = recv_ref[0, 48:, :].astype(F32)
    for p in range(1, peers):
        total = total + recv_ref[p, 48:, :].astype(F32)
    total = total.astype(BF16)
    for p in range(sum_ref.shape[0]):
        sum_ref[p] = total


def add_kernel(scale, recv_ref, out_ref):
    total = recv_ref[0].astype(F32)
    for p in range(1, recv_ref.shape[0]):
        total = total + recv_ref[p].astype(F32)
    total = (total * scale).astype(BF16)
    for p in range(out_ref.shape[0]):
        out_ref[p] = total


def finish_kernel(
    recv_ref, from_above_ref, from_below_ref, d_node_ref, fresh_ref, intra_ref, bound_ref,
    pick_ref, first_ref, second_ref, d_out_ref, coarse_ref,
):
    peers, _, feature = recv_ref.shape
    cells = d_node_ref.shape[0]
    head = recv_ref[:, 0:16, :].astype(F32)
    own = head[:, 0:8, :].reshape(8 * peers, feature).astype(BF16)
    hot = onehot_rows(column_of(intra_ref[...]), cells)
    total = mm_tn(hot, own)
    for k, back_ref in ((0, from_below_ref), (1, from_above_ref)):
        column = face_column(bound_ref[k : k + 1, :], pick_ref[k])
        total = total + mm_tn(onehot_rows(column, cells), back_ref[...])
    d_out_ref[...] = d_node_ref[...] + total
    partners = recv_ref[:, 32:48, :].reshape(16 * peers, feature)
    coarse = coarse_ref.shape[0]
    cell_row = iota((cells, coarse), 0)
    near = onehot((first_ref[...] == cell_row) | (second_ref[...] == cell_row))
    far = onehot(second_ref[...] - cells == iota((16 * peers, coarse), 0))
    coarse_ref[...] = (0.5 * (mm_tn(near, fresh_ref[...]) + mm_tn(far, partners))).astype(BF16)


def unpack_kernel(recv_ref, w1_ref, w2_ref, nw1_ref, nw2_ref, b1_ref, g_ref, nb1_ref, ng_ref):
    for p in range(3):
        w1_ref[128 * p : 128 * p + 128, :] = recv_ref[p].astype(F32)
    w2_ref[...] = recv_ref[3].astype(F32)
    nw1_ref[0:128, :] = recv_ref[4].astype(F32)
    nw1_ref[128:256, :] = recv_ref[5].astype(F32)
    nw2_ref[...] = recv_ref[6].astype(F32)
    tail = recv_ref[7, 0:16, :].astype(F32)
    b1_ref[...] = tail[0:1, :]
    g_ref[...] = tail[1:2, :]
    nb1_ref[...] = tail[2:3, :]
    ng_ref[...] = tail[3:4, :]


def call(kernel, out_shape, *args, scratch=(), smem=(), name=None, cost=None):
    specs = [
        pl.BlockSpec(memory_space=pltpu.SMEM if i in smem else pltpu.VMEM) for i in range(len(args))
    ]
    return pl.pallas_call(
        kernel,
        out_shape=out_shape,
        in_specs=specs,
        out_specs=jax.tree.map(lambda _: pl.BlockSpec(memory_space=pltpu.VMEM), out_shape),
        scratch_shapes=list(scratch),
        compiler_params=pltpu.CompilerParams(vmem_limit_bytes=VMEM_LIMIT),
        name=name,
        cost_estimate=cost,
    )(*args)


def shape_of(shape, dtype):
    return jax.ShapeDtypeStruct(shape, dtype)


def per_device(
    slabs, node, edges, edge_src, edge_dst, edge_count, intra_idx, bound_idx, cross_pick,
    match_send, pool_first, pool_second, edge_w1, edge_b1, edge_w2, edge_gain,
    node_w1, node_b1, node_w2, node_gain, edge_cot, coarse_cot,
):
    node, edges, edge_cot, coarse_cot = node[0, 0], edges[0, 0], edge_cot[0, 0], coarse_cot[0, 0]
    intra, bound, pick, match = intra_idx[0, 0], bound_idx[0, 0], cross_pick[0], match_send[0, 0]
    first, second = pool_first[0], pool_second[0]
    src, dst = edge_src[0], edge_dst[0]
    cells, feature = node.shape
    slots = edges.shape[0]
    coarse = coarse_cot.shape[0]
    peers = lax.axis_size("sub")
    planes, columns = lax.axis_size("z"), lax.axis_size("y")
    dom = ("z", "y")
    upward = [(i, i + 1) for i in range(slabs - 1)]
    downward = [(i + 1, i) for i in range(slabs - 1)]
    face = shape_of((8 * peers, feature), BF16)
    wide = -(-(cells + 24 * peers) // 256) * 256

    to_down, to_up = call(face_kernel, (face, face), node, bound, pick, name="faces")
    from_below = lax.ppermute(to_up, dom, upward)
    from_above = lax.ppermute(to_down, dom, downward)
    sent = call(
        send_kernel, shape_of((peers, ROWS_ONE, feature), BF16),
        node, intra, second, coarse_cot, from_below, from_above, name="send",
    )
    received = lax.all_to_all(sent, "sub", split_axis=0, concat_axis=0, tiled=True)

    new_edges, d_edges, d_node, fresh, sent = call(
        main_kernel,
        (
            shape_of((slots, feature), BF16),
            shape_of((slots, feature), BF16),
            shape_of((cells, feature), F32),
            shape_of((cells, feature), BF16),
            shape_of((peers, ROWS_TWO, feature), BF16),
        ),
        edge_count, src, dst, node, received, edges, edge_cot, coarse_cot, first, second, match,
        edge_w1, edge_b1[None], edge_w2, edge_gain[None],
        node_w1, node_b1[None], node_w2, node_gain[None],
        smem=(0,),
        scratch=(
            pltpu.VMEM((wide, feature), BF16),
            pltpu.VMEM((wide + cells, 2 * feature), BF16),
            pltpu.VMEM((slots, cells), BF16),
            pltpu.VMEM((cells, slots), BF16),
            pltpu.VMEM((cells, 2 * feature), F32),
            pltpu.VMEM((slots, feature), BF16),
            pltpu.VMEM((slots, feature), F32),
            pltpu.VMEM((slots, feature), F32),
            pltpu.VMEM((slots, 1), F32),
            pltpu.VMEM((cells, 2 * feature), BF16),
            pltpu.VMEM((wide + cells, feature), F32),
            pltpu.VMEM((feature, feature), F32),
            pltpu.VMEM((feature, feature), F32),
            pltpu.VMEM((8, feature), F32),
            pltpu.VMEM((8, feature), F32),
            pltpu.VMEM((peers * GRAD_ROWS, feature), F32),
        ),
        name="layer",
    )
    received = lax.all_to_all(sent, "sub", split_axis=0, concat_axis=0, tiled=True)
    piece = (GRAD_ROWS, feature)
    back_down, back_up, partial = call(
        split_kernel, (face, face, shape_of((planes,) + piece, BF16)), received, name="split"
    )
    from_above = lax.ppermute(back_down, dom, downward)
    from_below = lax.ppermute(back_up, dom, upward)
    partial = lax.all_to_all(partial, "z", split_axis=0, concat_axis=0, tiled=True)
    d_node, coarse_out = call(
        finish_kernel,
        (shape_of((cells, feature), F32), shape_of((coarse, feature), BF16)),
        received, from_above, from_below, d_node, fresh, intra, bound, pick, first, second,
        name="finish",
        cost=pl.CostEstimate(flops=300_000_000, bytes_accessed=2_000_000, transcendentals=0),
    )
    partial = call(
        functools.partial(add_kernel, 1.0), shape_of((columns,) + piece, BF16), partial, name="add_z"
    )
    partial = lax.all_to_all(partial, "y", split_axis=0, concat_axis=0, tiled=True)
    scale = 1.0 / math.sqrt(slabs * peers * slots)
    partial = call(
        functools.partial(add_kernel, scale), shape_of((peers,) + piece, BF16), partial, name="add_y"
    )
    grads = lax.all_to_all(partial, "sub", split_axis=0, concat_axis=0, tiled=True)
    row = shape_of((1, feature), F32)
    w1, w2, nw1, nw2, b1, g, nb1, ng = call(
        unpack_kernel,
        (
            shape_of((3 * feature, feature), F32),
            shape_of((feature, feature), F32),
            shape_of((2 * feature, feature), F32),
            shape_of((feature, feature), F32),
            row, row, row, row,
        ),
        grads,
        name="unpack",
    )
    return (
        new_edges[None, None], coarse_out[None, None], d_node[None, None], d_edges[None, None],
        w1, b1[0], w2, g[0], nw1, nb1[0], nw2, ng[0],
    )


def solution(mesh):
    slabs, peers = mesh.shape["dom"], mesh.shape["sub"]
    columns = 4 if slabs % 8 == 0 else 2
    inner = Mesh(mesh.devices.reshape(slabs // columns, columns, peers), ("z", "y", "sub"))
    dom = ("z", "y")
    four, three = P(dom, "sub", None, None), P(dom, "sub", None)
    return jax.shard_map(
        functools.partial(per_device, slabs),
        mesh=inner,
        in_specs=(
            four, four, three, three, P(dom, "sub"), four, four, P("sub", None, None, None),
            four, three, three, P(), P(), P(), P(), P(), P(), P(), P(), four, four,
        ),
        out_specs=(four, four, four, four) + (P(),) * 8,
        check_vma=False,
    )
```

```python
import functools
import math

import jax
import jax.numpy as jnp
from jax import lax
from jax.experimental import pallas as pl
from jax.experimental.pallas import tpu as pltpu
from jax.sharding import Mesh
from jax.sharding import PartitionSpec as P

NORM_EPSILON = 1e-05
F32 = jnp.float32
BF16 = jnp.bfloat16
TILE = 256
MIB = 1024 * 1024

PAIR = ("y0", "sub")
PLANE = ("y1", "y0", "sub")
HEAD = 32
GRAD_ROWS = 1024


def mm(a, b):
    return lax.dot_general(a, b, (((1,), (0,)), ((), ())), preferred_element_type=F32)


def mm_nt(a, b):
    return lax.dot_general(a, b, (((1,), (1,)), ((), ())), preferred_element_type=F32)


def mm_tn(a, b):
    return lax.dot_general(a, b, (((0,), (0,)), ((), ())), preferred_element_type=F32)


def iota(shape, dim):
    return lax.broadcasted_iota(jnp.int32, shape, dim)


def onehot(mask):
    return jnp.where(mask, 1.0, 0.0).astype(BF16)


def two_parts(x):
    high = x.astype(BF16)
    low = (x - high.astype(F32)).astype(BF16)
    return high, low


def column_of(ids):
    a, b = ids.shape
    spread = jnp.broadcast_to(ids[:, None, :], (a, b, b))
    keep = iota((a, b, b), 1) == iota((a, b, b), 2)
    return jnp.sum(jnp.where(keep, spread, 0), axis=2, keepdims=True).reshape(a * b, 1)


def face_column(face_row, pick):
    spot = column_of(pick)
    shape = (spot.shape[0], face_row.shape[1])
    keep = spot == iota(shape, 1)
    return jnp.sum(jnp.where(keep, jnp.broadcast_to(face_row, shape), 0), axis=1, keepdims=True)


def onehot_rows(column, width):
    return onehot(column == iota((column.shape[0], width), 1))


def slab_in_plane():
    return lax.axis_index("y1") * lax.axis_size("y0") + lax.axis_index("y0")


def picked_rows(node, bound_ref, pick_ref, side):
    face_row = jnp.where(side == 0, bound_ref[0:1, :], bound_ref[1:2, :])
    return mm(onehot_rows(face_column(face_row, pick_ref[side]), node.shape[0]), node)


def face_kernel(node_ref, bound_ref, pick_ref, out_ref):
    out_ref[...] = picked_rows(node_ref[...], bound_ref, pick_ref, lax.axis_index("y0")).astype(BF16)


def send_kernel(node_ref, intra_ref, second_ref, coarse_cot_ref, bound_ref, pick_ref, out_ref):
    odd = lax.axis_index("y0")
    node = node_ref[...]
    cells, feature = node.shape
    peers, halo = intra_ref.shape
    coarse = coarse_cot_ref.shape[0]
    intra = mm(onehot_rows(column_of(intra_ref[...]), cells), node)
    half = 0.5 * coarse_cot_ref[...].astype(F32)
    pool_rows = 16 * peers
    pool = mm(onehot(second_ref[...] - cells == iota((pool_rows, coarse), 0)), half.astype(BF16))
    same = [
        intra.reshape(peers, halo, feature),
        jnp.zeros((peers, halo, feature), F32),
        pool.reshape(peers, 16, feature),
    ]
    other = [
        picked_rows(node, bound_ref, pick_ref, 1 - odd).reshape(peers, halo, feature),
        jnp.zeros((peers, HEAD - halo, feature), F32),
    ]
    out_ref[pl.ds(peers * odd, peers)] = jnp.concatenate(same, axis=1).astype(BF16)
    out_ref[pl.ds(peers * (1 - odd), peers)] = jnp.concatenate(other, axis=1).astype(BF16)


def silu_parts(pre):
    sig = 0.5 * jnp.tanh(0.5 * pre) + 0.5
    act = (pre * sig).astype(BF16)
    slope = sig * (1.0 + pre * (1.0 - sig))
    return act, slope


def norm_forward(out):
    centred = out - jnp.mean(out, axis=1, keepdims=True)
    inv = lax.rsqrt(jnp.mean(centred * centred, axis=1, keepdims=True) + NORM_EPSILON)
    return centred * inv, inv


def norm_backward(u, normed, inv, gain):
    scaled = u * gain
    inner = (
        scaled
        - jnp.mean(scaled, axis=1, keepdims=True)
        - normed * jnp.mean(scaled * normed, axis=1, keepdims=True)
    )
    return inner * inv


def fold_rows(x):
    rows, feature = x.shape
    return jnp.sum(x.reshape(rows // 8, 8, feature), axis=0)


def main_kernel(
    count_ref, src_ref, dst_ref, node_ref, recv_ref, edges_ref, cot_ref, coarse_cot_ref,
    first_ref, second_ref, match_ref, ew1_ref, eb1_ref, ew2_ref, eg_ref,
    nw1_ref, nb1_ref, nw2_ref, ng_ref,
    new_edges_ref, d_edges_ref, d_node_ref, fresh_ref, send_ref,
    table_ref, t2_ref, ohd_ref, oht_ref, agg_ref, act_ref, slope_ref, normed_ref, inv_ref,
    dagg_ref, s_ref, dw1_ref, dw2_ref, db1_ref, dg_ref, grads_ref,
):
    cells, feature = node_ref.shape
    slots = edges_ref.shape[0]
    peers = recv_ref.shape[0] // 2
    tiles = slots // TILE
    count = count_ref[0, 0]
    node = node_ref[...]
    odd = lax.axis_index("y0")
    same = recv_ref[pl.ds(peers * odd, peers)]
    near = same.astype(F32)
    other = recv_ref[pl.ds(peers * (1 - odd), peers)].astype(F32)[:, 0:8, :]
    passed = near[:, 8:16, :]
    kinds = [near[:, 0:8, :], jnp.where(odd == 0, passed, other), jnp.where(odd == 0, other, passed)]
    halo_rows = 3 * 8 * peers
    wide = table_ref.shape[0]
    table_ref[0:cells, :] = node
    halo = jnp.concatenate(
        [rows.reshape(8 * peers, feature) for rows in kinds]
        + [jnp.zeros((wide - cells - halo_rows, feature), F32)],
        axis=0,
    )
    table_ref[cells:wide, :] = halo.astype(BF16)
    ew1_edge = ew1_ref[0:feature, :]
    ew1_src = ew1_ref[feature : 2 * feature, :]
    ew1_dst = ew1_ref[2 * feature : 3 * feature, :]
    high, low = two_parts(mm(table_ref[...], ew1_src))
    t2_ref[0:wide, 0:feature] = high
    t2_ref[0:wide, feature:] = low
    high, low = two_parts(mm(node, ew1_dst) + eb1_ref[...])
    t2_ref[wide:, 0:feature] = high
    t2_ref[wide:, feature:] = low
    agg_ref[...] = jnp.zeros_like(agg_ref)
    ew2 = ew2_ref[...]
    eg = eg_ref[...]

    def live_of(start):
        return iota((TILE, feature), 0) + start < count

    def forward_tile(i, carry):
        start = pl.multiple_of(i * TILE, TILE)
        rows = pl.ds(start, TILE)
        src = src_ref[:, rows]
        dst = dst_ref[:, rows]
        src_col = jnp.broadcast_to(src, (128, TILE)).T
        dst_col = jnp.broadcast_to(dst, (128, TILE)).T
        lane = iota((TILE, 128), 1)
        hot_src = jnp.concatenate(
            [onehot(src_col == lane + 128 * k) for k in range(wide // 128)], axis=1
        )
        hot_dst = jnp.concatenate(
            [onehot(dst_col == lane + 128 * k) for k in range(cells // 128)], axis=1
        )
        ohd_ref[rows, :] = hot_dst
        both = mm(hot_src, t2_ref[0:wide, :]) + mm(hot_dst, t2_ref[wide:, :])
        edges = edges_ref[rows, :]
        pre = both[:, 0:feature] + both[:, feature:] + mm(edges, ew1_edge)
        act, slope = silu_parts(pre)
        act_ref[rows, :] = act
        slope_ref[rows, :] = slope
        normed, inv = norm_forward(mm(act, ew2))
        normed_ref[rows, :] = normed
        inv_ref[rows, :] = inv
        live = live_of(start)
        message = jnp.where(live, normed * eg, 0.0)
        new_edges_ref[rows, :] = jnp.where(live, edges.astype(F32) + message, 0.0).astype(BF16)
        hot = onehot(dst == iota((cells, TILE), 0))
        oht_ref[:, rows] = hot
        agg_ref[...] += mm(hot, jnp.concatenate(two_parts(message), axis=1))
        return carry

    lax.fori_loop(0, tiles, forward_tile, 0)

    aggregate = (agg_ref[:, 0:feature] + agg_ref[:, feature:]).astype(BF16)
    nw1_node = nw1_ref[0:feature, :]
    nw1_agg = nw1_ref[feature:, :]
    pre = mm(node, nw1_node) + mm(aggregate, nw1_agg) + nb1_ref[...]
    act, slope = silu_parts(pre)
    nw2 = nw2_ref[...]
    ng = ng_ref[...]
    normed, inv = norm_forward(mm(act, nw2))
    fresh = (node.astype(F32) + normed * ng).astype(BF16)
    fresh_ref[...] = fresh

    coarse = coarse_cot_ref.shape[0]
    half = (0.5 * coarse_cot_ref[...].astype(F32)).astype(BF16)
    cell_row = iota((cells, coarse), 0)
    pooled = onehot((first_ref[...] == cell_row) | (second_ref[...] == cell_row))
    returned = same[:, 16:32, :].reshape(16 * peers, feature)
    hot_match = onehot_rows(column_of(match_ref[...]), cells)
    d_fresh = mm(pooled, half) + mm_tn(hot_match, returned)
    match_rows = mm(hot_match, fresh)

    d_out = norm_backward(d_fresh, normed, inv, ng)
    grads_ref[899:900, :] = jnp.sum(d_fresh * normed, axis=0, keepdims=True)
    d_out_half = d_out.astype(BF16)
    grads_ref[768:896, :] = mm_tn(act, d_out_half)
    d_pre = mm_nt(d_out_half, nw2) * slope
    grads_ref[898:899, :] = jnp.sum(d_pre, axis=0, keepdims=True)
    d_pre_half = d_pre.astype(BF16)
    grads_ref[512:640, :] = mm_tn(node, d_pre_half)
    grads_ref[640:768, :] = mm_tn(aggregate, d_pre_half)
    d_node_ref[...] = d_fresh + mm_nt(d_pre_half, nw1_node)
    high, low = two_parts(mm_nt(d_pre_half, nw1_agg))
    dagg_ref[:, 0:feature] = high
    dagg_ref[:, feature:] = low

    s_ref[...] = jnp.zeros_like(s_ref)
    dw1_ref[...] = jnp.zeros_like(dw1_ref)
    dw2_ref[...] = jnp.zeros_like(dw2_ref)
    db1_ref[...] = jnp.zeros_like(db1_ref)
    dg_ref[...] = jnp.zeros_like(dg_ref)

    def backward_tile(i, carry):
        start = pl.multiple_of(i * TILE, TILE)
        rows = pl.ds(start, TILE)
        both = mm(ohd_ref[rows, :], dagg_ref[...])
        live = live_of(start)
        cot = jnp.where(live, cot_ref[rows, :].astype(F32), 0.0)
        u = jnp.where(live, cot + (both[:, 0:feature] + both[:, feature:]), 0.0)
        normed = normed_ref[rows, :]
        d_out_half = norm_backward(u, normed, inv_ref[rows, :], eg).astype(BF16)
        dg_ref[...] += fold_rows(u * normed)
        dw2_ref[...] += mm_tn(act_ref[rows, :], d_out_half)
        d_pre = mm_nt(d_out_half, ew2) * slope_ref[rows, :]
        db1_ref[...] += fold_rows(d_pre)
        d_pre_half = d_pre.astype(BF16)
        d_edges_ref[rows, :] = (cot + mm_nt(d_pre_half, ew1_edge)).astype(BF16)
        dw1_ref[...] += mm_tn(edges_ref[rows, :], d_pre_half)
        hot = onehot(src_ref[:, rows] == iota((wide, TILE), 0))
        s_ref[0:wide, :] += mm(hot, d_pre_half)
        s_ref[wide:, :] += mm(oht_ref[:, rows], d_pre_half)
        return carry

    lax.fori_loop(0, tiles, backward_tile, 0)

    grads_ref[0:128, :] = dw1_ref[...]
    grads_ref[384:512, :] = dw2_ref[...]
    grads_ref[896:897, :] = jnp.sum(db1_ref[...], axis=0, keepdims=True)
    grads_ref[897:898, :] = jnp.sum(dg_ref[...], axis=0, keepdims=True)
    grads_ref[900:, :] = jnp.zeros_like(grads_ref[900:, :])
    high, low = two_parts(s_ref[0:wide, :])
    table = table_ref[...]
    grads_ref[128:256, :] = mm_tn(table, high) + mm_tn(table, low)
    d_table = mm_nt(high, ew1_src) + mm_nt(low, ew1_src)
    high, low = two_parts(s_ref[wide:, :])
    grads_ref[256:384, :] = mm_tn(node, high) + mm_tn(node, low)
    d_node_ref[...] += d_table[0:cells, :] + (mm_nt(high, ew1_dst) + mm_nt(low, ew1_dst))
    kinds = [
        d_table[cells + 8 * peers * k : cells + 8 * peers * (k + 1), :].reshape(peers, 8, feature)
        for k in range(3)
    ]
    slab = slab_in_plane()
    slabs = send_ref.shape[0] // peers
    pad = [jnp.zeros((peers, HEAD - 8, feature), F32)]
    blank = jnp.zeros((peers, HEAD, feature), BF16)
    for y in range(slabs):
        send_ref[peers * y : peers * (y + 1), 0:HEAD, :] = blank
    onward = jnp.where(slab == 0, kinds[1], kinds[2])
    same = [kinds[0], onward, match_rows.reshape(peers, 16, feature)]
    send_ref[pl.ds(peers * slab, peers), 0:HEAD, :] = jnp.concatenate(same, axis=1).astype(BF16)

    @pl.when(slab > 0)
    def _():
        rows = jnp.concatenate([kinds[1]] + pad, axis=1).astype(BF16)
        send_ref[pl.ds(peers * (slab - 1), peers), 0:HEAD, :] = rows

    @pl.when(slab < slabs - 1)
    def _():
        rows = jnp.concatenate([kinds[2]] + pad, axis=1).astype(BF16)
        send_ref[pl.ds(peers * (slab + 1), peers), 0:HEAD, :] = rows

    share = GRAD_ROWS // (slabs * peers)
    grads = grads_ref[...].reshape(slabs * peers, share, feature)
    send_ref[:, HEAD:, :] = grads.astype(BF16)


def finish_kernel(
    recv_ref, passed_ref, d_node_ref, fresh_ref, intra_ref, bound_ref,
    pick_ref, first_ref, second_ref, d_out_ref, coarse_ref,
):
    peers = intra_ref.shape[0]
    slabs = recv_ref.shape[0] // peers
    cells, feature = d_node_ref.shape
    slab = slab_in_plane()
    same = recv_ref[pl.ds(peers * slab, peers), 0:HEAD, :]

    def gradients(block):
        return block.astype(F32)[:, 0:8, :].reshape(8 * peers, feature).astype(BF16)

    hot = onehot_rows(column_of(intra_ref[...]), cells)
    total = mm_tn(hot, gradients(same))
    passed = passed_ref[...]
    lower = jnp.maximum(slab - 1, 0)
    upper = jnp.minimum(slab + 1, slabs - 1)
    for k, near, edge in ((0, lower, slab == 0), (1, upper, slab == slabs - 1)):
        column = face_column(bound_ref[k : k + 1, :], pick_ref[k])
        direct = gradients(recv_ref[pl.ds(peers * near, peers), 0:HEAD, :])
        total = total + mm_tn(onehot_rows(column, cells), jnp.where(edge, passed, direct))
    d_out_ref[...] = d_node_ref[...] + total
    partners = same[:, 16:32, :].reshape(16 * peers, feature)
    coarse = coarse_ref.shape[0]
    cell_row = iota((cells, coarse), 0)
    near = onehot((first_ref[...] == cell_row) | (second_ref[...] == cell_row))
    far = onehot(second_ref[...] - cells == iota((16 * peers, coarse), 0))
    coarse_ref[...] = (0.5 * (mm_tn(near, fresh_ref[...]) + mm_tn(far, partners))).astype(BF16)


def unpack_kernel(recv_ref, w1_ref, w2_ref, nw1_ref, nw2_ref, b1_ref, g_ref, nb1_ref, ng_ref):
    start = 0
    for out_ref in (w1_ref, w2_ref, nw1_ref, nw2_ref):
        rows = out_ref.shape[0]
        out_ref[...] = recv_ref[start : start + rows, :].astype(F32)
        start += rows
    tail = recv_ref[start : start + 16, :].astype(F32)
    for k, out_ref in enumerate((b1_ref, g_ref, nb1_ref, ng_ref)):
        out_ref[...] = tail[k : k + 1, :]


def call(kernel, out_shape, *args, scratch=(), smem=(), name=None, cost=None, mib=8):
    specs = [
        pl.BlockSpec(memory_space=pltpu.SMEM if i in smem else pltpu.VMEM) for i in range(len(args))
    ]
    return pl.pallas_call(
        kernel,
        out_shape=out_shape,
        in_specs=specs,
        out_specs=jax.tree.map(lambda _: pl.BlockSpec(memory_space=pltpu.VMEM), out_shape),
        scratch_shapes=list(scratch),
        compiler_params=pltpu.CompilerParams(vmem_limit_bytes=mib * MIB),
        name=name,
        cost_estimate=cost,
    )(*args)


def shape_of(shape, dtype):
    return jax.ShapeDtypeStruct(shape, dtype)


def per_device(
    slabs, node, edges, edge_src, edge_dst, edge_count, intra_idx, bound_idx, cross_pick,
    match_send, pool_first, pool_second, edge_w1, edge_b1, edge_w2, edge_gain,
    node_w1, node_b1, node_w2, node_gain, edge_cot, coarse_cot,
):
    node, edges, edge_cot, coarse_cot = node[0, 0], edges[0, 0], edge_cot[0, 0], coarse_cot[0, 0]
    intra, bound, pick, match = intra_idx[0, 0], bound_idx[0, 0], cross_pick[0], match_send[0, 0]
    first, second = pool_first[0], pool_second[0]
    src, dst = edge_src[0], edge_dst[0]
    cells, feature = node.shape
    slots = edges.shape[0]
    coarse = coarse_cot.shape[0]
    peers = lax.axis_size("sub")
    planes = lax.axis_size("z")
    in_plane = slabs // planes
    dom = ("z", "y1", "y0")
    face = shape_of((8 * peers, feature), BF16)
    wide = -(-(cells + 24 * peers) // 256) * 256

    def swap(rows, step):
        pairs = [(i - 1, i) for i in range(step, slabs, step)]
        return lax.ppermute(rows, dom, pairs + [(j, i) for i, j in pairs])

    def exchange(blocks, axes):
        return lax.all_to_all(blocks, axes, split_axis=0, concat_axis=0, tiled=True)

    passed = swap(call(face_kernel, face, node, bound, pick, name="faces"), 2)
    sent = call(
        send_kernel, shape_of((2 * peers, HEAD, feature), BF16),
        node, intra, second, coarse_cot, bound, pick, name="send",
        cost=pl.CostEstimate(flops=60_000_000, bytes_accessed=400_000, transcendentals=0),
    )
    sent = lax.dynamic_update_slice(
        sent, passed.reshape(peers, 8, feature), (peers * lax.axis_index("y0"), 8, 0)
    )
    received = exchange(sent, PAIR)

    new_edges, d_edges, d_node, fresh, sent = call(
        main_kernel,
        (
            shape_of((slots, feature), BF16),
            shape_of((slots, feature), BF16),
            shape_of((cells, feature), F32),
            shape_of((cells, feature), BF16),
            shape_of((in_plane * peers, HEAD + GRAD_ROWS // (in_plane * peers), feature), BF16),
        ),
        edge_count, src, dst, node, received, edges, edge_cot, coarse_cot, first, second, match,
        edge_w1, edge_b1[None], edge_w2, edge_gain[None],
        node_w1, node_b1[None], node_w2, node_gain[None],
        smem=(0,),
        scratch=(
            pltpu.VMEM((wide, feature), BF16),
            pltpu.VMEM((wide + cells, 2 * feature), BF16),
            pltpu.VMEM((slots, cells), BF16),
            pltpu.VMEM((cells, slots), BF16),
            pltpu.VMEM((cells, 2 * feature), F32),
            pltpu.VMEM((slots, feature), BF16),
            pltpu.VMEM((slots, feature), F32),
            pltpu.VMEM((slots, feature), F32),
            pltpu.VMEM((slots, 1), F32),
            pltpu.VMEM((cells, 2 * feature), BF16),
            pltpu.VMEM((wide + cells, feature), F32),
            pltpu.VMEM((feature, feature), F32),
            pltpu.VMEM((feature, feature), F32),
            pltpu.VMEM((8, feature), F32),
            pltpu.VMEM((8, feature), F32),
            pltpu.VMEM((GRAD_ROWS, feature), F32),
        ),
        name="layer",
        mib=24,
    )
    received = exchange(sent, PLANE)
    onward = lax.dynamic_slice(received, (peers * slab_in_plane(), 8, 0), (peers, 8, feature))
    passed = swap(onward.reshape(8 * peers, feature), in_plane)
    scale = 1.0 / math.sqrt(slabs * peers * slots)

    def total(blocks, factor, copies):
        rows = (jnp.sum(blocks.astype(F32), axis=0) * factor).astype(BF16)
        return jnp.broadcast_to(rows, (copies,) + rows.shape)

    summed = exchange(total(received[:, HEAD:], 1.0, planes), "z")
    grads = exchange(total(summed, scale, in_plane * peers), PLANE)
    d_node, coarse_out = call(
        finish_kernel,
        (shape_of((cells, feature), F32), shape_of((coarse, feature), BF16)),
        received, passed, d_node, fresh, intra, bound, pick, first, second,
        name="finish",
        cost=pl.CostEstimate(flops=300_000_000, bytes_accessed=2_000_000, transcendentals=0),
    )
    row = shape_of((1, feature), F32)
    w1, w2, nw1, nw2, b1, g, nb1, ng = call(
        unpack_kernel,
        (
            shape_of((3 * feature, feature), F32),
            shape_of((feature, feature), F32),
            shape_of((2 * feature, feature), F32),
            shape_of((feature, feature), F32),
            row, row, row, row,
        ),
        grads.reshape(GRAD_ROWS, feature),
        name="unpack",
    )
    return (
        new_edges[None, None], coarse_out[None, None], d_node[None, None], d_edges[None, None],
        w1, b1[0], w2, g[0], nw1, nb1[0], nw2, ng[0],
    )


def solution(mesh):
    slabs, peers = mesh.shape["dom"], mesh.shape["sub"]
    devices = mesh.devices.reshape(slabs // 4, 2, 2, peers)
    dom = ("z", "y1", "y0")
    inner = Mesh(devices, dom + ("sub",))
    four, three = P(dom, "sub", None, None), P(dom, "sub", None)
    return jax.shard_map(
        functools.partial(per_device, slabs),
        mesh=inner,
        in_specs=(
            four, four, three, three, P(dom, "sub"), four, four, P("sub", None, None, None),
            four, three, three, P(), P(), P(), P(), P(), P(), P(), P(), four, four,
        ),
        out_specs=(four, four, four, four) + (P(),) * 8,
        check_vma=False,
    )
```

```python
import functools
import math

import jax
import jax.numpy as jnp
from jax import lax
from jax.experimental import pallas as pl
from jax.experimental.pallas import tpu as pltpu
from jax.sharding import Mesh
from jax.sharding import PartitionSpec as P

NORM_EPSILON = 1e-05
F32 = jnp.float32
BF16 = jnp.bfloat16
TILE = 2048
UNROLL = 1
MIB = 1024 * 1024

PAIR = ("y0", "sub")
PLANE = ("y1", "y0", "sub")
HEAD = 32
GRAD_ROWS = 1024


def mm(a, b):
    return lax.dot_general(a, b, (((1,), (0,)), ((), ())), preferred_element_type=F32)


def mm_nt(a, b):
    return lax.dot_general(a, b, (((1,), (1,)), ((), ())), preferred_element_type=F32)


def mm_tn(a, b):
    return lax.dot_general(a, b, (((0,), (0,)), ((), ())), preferred_element_type=F32)


def iota(shape, dim):
    return lax.broadcasted_iota(jnp.int32, shape, dim)


def onehot(mask):
    return jnp.where(mask, 1.0, 0.0).astype(BF16)


def two_parts(x):
    high = x.astype(BF16)
    low = (x - high.astype(F32)).astype(BF16)
    return high, low


def column_of(ids):
    a, b = ids.shape
    spread = jnp.broadcast_to(ids[:, None, :], (a, b, b))
    keep = iota((a, b, b), 1) == iota((a, b, b), 2)
    return jnp.sum(jnp.where(keep, spread, 0), axis=2, keepdims=True).reshape(a * b, 1)


def face_column(face_row, pick):
    spot = column_of(pick)
    shape = (spot.shape[0], face_row.shape[1])
    keep = spot == iota(shape, 1)
    return jnp.sum(jnp.where(keep, jnp.broadcast_to(face_row, shape), 0), axis=1, keepdims=True)


def onehot_rows(column, width):
    return onehot(column == iota((column.shape[0], width), 1))


def slab_in_plane():
    return lax.axis_index("y1") * lax.axis_size("y0") + lax.axis_index("y0")


def picked_rows(node, bound_ref, pick_ref, side):
    face_row = jnp.where(side == 0, bound_ref[0:1, :], bound_ref[1:2, :])
    return mm(onehot_rows(face_column(face_row, pick_ref[side]), node.shape[0]), node)


def face_kernel(node_ref, bound_ref, pick_ref, out_ref):
    out_ref[...] = picked_rows(node_ref[...], bound_ref, pick_ref, lax.axis_index("y0")).astype(BF16)


def send_kernel(node_ref, intra_ref, second_ref, coarse_cot_ref, bound_ref, pick_ref, out_ref):
    odd = lax.axis_index("y0")
    node = node_ref[...]
    cells, feature = node.shape
    peers, halo = intra_ref.shape
    coarse = coarse_cot_ref.shape[0]
    intra = mm(onehot_rows(column_of(intra_ref[...]), cells), node)
    half = 0.5 * coarse_cot_ref[...].astype(F32)
    pool_rows = 16 * peers
    pool = mm(onehot(second_ref[...] - cells == iota((pool_rows, coarse), 0)), half.astype(BF16))
    same = [
        intra.reshape(peers, halo, feature),
        jnp.zeros((peers, halo, feature), F32),
        pool.reshape(peers, 16, feature),
    ]
    other = [
        picked_rows(node, bound_ref, pick_ref, 1 - odd).reshape(peers, halo, feature),
        jnp.zeros((peers, HEAD - halo, feature), F32),
    ]
    out_ref[pl.ds(peers * odd, peers)] = jnp.concatenate(same, axis=1).astype(BF16)
    out_ref[pl.ds(peers * (1 - odd), peers)] = jnp.concatenate(other, axis=1).astype(BF16)


def silu_parts(pre):
    sig = 0.5 * jnp.tanh(0.5 * pre) + 0.5
    act = (pre * sig).astype(BF16)
    slope = sig * (1.0 + pre * (1.0 - sig))
    return act, slope


def norm_forward(out, axis):
    centred = out - jnp.mean(out, axis=axis, keepdims=True)
    inv = lax.rsqrt(jnp.mean(centred * centred, axis=axis, keepdims=True) + NORM_EPSILON)
    return centred * inv, inv


def norm_backward(u, normed, inv, gain, axis):
    scaled = u * gain
    inner = (
        scaled
        - jnp.mean(scaled, axis=axis, keepdims=True)
        - normed * jnp.mean(scaled * normed, axis=axis, keepdims=True)
    )
    return inner * inv


def fold_lanes(x):
    total = x[:, 0:128]
    for k in range(1, x.shape[1] // 128):
        total = total + x[:, 128 * k : 128 * k + 128]
    return total


def column_block(row, width):
    block = jnp.broadcast_to(row, (128, 128)).T
    return jnp.concatenate([block] * (width // 128), axis=1)


def hot_columns(ids, rows):
    width = ids.shape[1]

    def spread(x):
        return jnp.broadcast_to(x.astype(F32), (16, width)).astype(BF16)

    tens, units = spread(ids & -16), spread(ids & 15)
    zero = jnp.zeros((16, width), BF16)
    base = jnp.where(units == iota((16, width), 0).astype(F32).astype(BF16), jnp.ones((16, width), BF16), zero)
    return jnp.concatenate(
        [jnp.where(tens == jnp.full((16, width), 16 * r, BF16), base, zero) for r in range(rows // 16)], axis=0
    )


def main_kernel(
    count_ref, recv_ref,
    src_in, dst_in, node_in, ew1_in, edges_in, eb1_in, ew2_in, eg_in,
    coarse_in, first_in, second_in, match_in, nw1_in, nb1_in, nw2_in, ng_in, cot_in,
    new_edges_out, d_edges_out, d_node_ref, fresh_ref, send_ref,
    src_ref, dst_ref, node_ref, ew1_ref, edges_ref, eb1_ref, ew2_ref, eg_ref,
    coarse_cot_ref, first_ref, second_ref, match_ref, nw1_ref, nb1_ref, nw2_ref, ng_ref, cot_ref,
    new_edges_ref, d_edges_ref,
    table_ref, t2_ref, oht_ref, agg_ref, act_ref, slope_ref, normed_ref, inv_ref,
    dagg_ref, s_ref, dw1_ref, dw2_ref, db1_ref, dg_ref, grads_ref, in_sem, out_sem,
):
    sources = (
        src_in, dst_in, node_in, ew1_in, edges_in, eb1_in, ew2_in, eg_in,
        coarse_in, first_in, second_in, match_in, nw1_in, nb1_in, nw2_in, ng_in, cot_in,
    )
    targets = (
        src_ref, dst_ref, node_ref, ew1_ref, edges_ref, eb1_ref, ew2_ref, eg_ref,
        coarse_cot_ref, first_ref, second_ref, match_ref, nw1_ref, nb1_ref, nw2_ref, ng_ref, cot_ref,
    )
    copies = [
        pltpu.make_async_copy(source, target, in_sem.at[k])
        for k, (source, target) in enumerate(zip(sources, targets))
    ]
    for copy in copies:
        copy.start()
    for copy in copies[:8]:
        copy.wait()
    cells, feature = node_ref.shape
    slots = edges_ref.shape[0]
    peers = recv_ref.shape[0] // 2
    tiles = slots // TILE
    count = count_ref[0, 0]
    node = node_ref[...]
    odd = lax.axis_index("y0")
    same = recv_ref[pl.ds(peers * odd, peers)]
    near = same.astype(F32)
    other = recv_ref[pl.ds(peers * (1 - odd), peers)].astype(F32)[:, 0:8, :]
    passed = near[:, 8:16, :]
    kinds = [near[:, 0:8, :], jnp.where(odd == 0, passed, other), jnp.where(odd == 0, other, passed)]
    halo_rows = 3 * 8 * peers
    wide = table_ref.shape[0]
    table_ref[0:cells, :] = node
    halo = jnp.concatenate(
        [rows.reshape(8 * peers, feature) for rows in kinds]
        + [jnp.zeros((wide - cells - halo_rows, feature), F32)],
        axis=0,
    )
    table_ref[cells:wide, :] = halo.astype(BF16)
    ew1_edge_t = ew1_ref[0:feature, :].T
    ew1_src = ew1_ref[feature : 2 * feature, :]
    ew1_dst = ew1_ref[2 * feature : 3 * feature, :]
    high, low = two_parts(mm_nt(ew1_src.T, table_ref[...]))
    t2_ref[0:feature, 0:wide] = high
    t2_ref[feature:, 0:wide] = low
    high, low = two_parts(mm_nt(ew1_dst.T, node) + column_block(eb1_ref[...], cells))
    t2_ref[0:feature, wide:] = high
    t2_ref[feature:, wide:] = low
    agg_ref[...] = jnp.zeros_like(agg_ref)
    ew2 = ew2_ref[...]
    ew2_t = ew2.T
    eg = column_block(eg_ref[...], TILE)

    def forward_tile(i, carry):
        start = pl.multiple_of(i * TILE, TILE)
        rows = pl.ds(start, TILE)
        hot_src = hot_columns(src_ref[:, rows], wide)
        hot_dst = hot_columns(dst_ref[:, rows], cells)
        oht_ref[0:wide, rows] = hot_src
        oht_ref[wide:, rows] = hot_dst
        both = mm(t2_ref[:, 0:wide], hot_src) + mm(t2_ref[:, wide:], hot_dst)
        edges = edges_ref[rows, :]
        pre = both[0:feature] + both[feature:] + mm_nt(ew1_edge_t, edges)
        act, slope = silu_parts(pre)
        act_ref[:, rows] = act
        slope_ref[:, rows] = slope
        normed, inv = norm_forward(mm(ew2_t, act), 0)
        normed_ref[:, rows] = normed
        inv_ref[:, rows] = inv
        message = jnp.where(iota((feature, TILE), 1) + start < count, normed * eg, 0.0)
        fresh_edges = jnp.where(
            iota((TILE, feature), 0) + start < count, edges.astype(F32) + message.T, 0.0
        )
        new_edges_ref[rows, :] = fresh_edges.astype(BF16)
        agg_ref[...] += mm_nt(hot_dst, jnp.concatenate(two_parts(message), axis=0))
        return carry

    lax.fori_loop(0, tiles, forward_tile, 0, unroll=UNROLL)
    edges_copy = pltpu.make_async_copy(new_edges_ref, new_edges_out, out_sem.at[0])
    edges_copy.start()
    for copy in copies[8:]:
        copy.wait()

    aggregate = (agg_ref[:, 0:feature] + agg_ref[:, feature:]).astype(BF16)
    nw1_node = nw1_ref[0:feature, :]
    nw1_agg = nw1_ref[feature:, :]
    pre = mm(node, nw1_node) + mm(aggregate, nw1_agg) + nb1_ref[...]
    act, slope = silu_parts(pre)
    nw2 = nw2_ref[...]
    ng = ng_ref[...]
    normed, inv = norm_forward(mm(act, nw2), 1)
    fresh = (node.astype(F32) + normed * ng).astype(BF16)
    fresh_ref[...] = fresh

    coarse = coarse_cot_ref.shape[0]
    half = (0.5 * coarse_cot_ref[...].astype(F32)).astype(BF16)
    cell_row = iota((cells, coarse), 0)
    pooled = onehot((first_ref[...] == cell_row) | (second_ref[...] == cell_row))
    returned = same[:, 16:32, :].reshape(16 * peers, feature)
    hot_match = onehot_rows(column_of(match_ref[...]), cells)
    d_fresh = mm(pooled, half) + mm_tn(hot_match, returned)
    match_rows = mm(hot_match, fresh)

    d_out = norm_backward(d_fresh, normed, inv, ng, 1)
    grads_ref[899:900, :] = jnp.sum(d_fresh * normed, axis=0, keepdims=True)
    d_out_half = d_out.astype(BF16)
    grads_ref[768:896, :] = mm_tn(act, d_out_half)
    d_pre = mm_nt(d_out_half, nw2) * slope
    grads_ref[898:899, :] = jnp.sum(d_pre, axis=0, keepdims=True)
    d_pre_half = d_pre.astype(BF16)
    grads_ref[512:640, :] = mm_tn(node, d_pre_half)
    grads_ref[640:768, :] = mm_tn(aggregate, d_pre_half)
    d_node_ref[...] = d_fresh + mm_nt(d_pre_half, nw1_node)
    high, low = two_parts(mm_nt(nw1_agg, d_pre_half))
    dagg_ref[0:feature, :] = high
    dagg_ref[feature:, :] = low

    s_ref[...] = jnp.zeros_like(s_ref)
    dw1_ref[...] = jnp.zeros_like(dw1_ref)
    dw2_ref[...] = jnp.zeros_like(dw2_ref)
    db1_ref[...] = jnp.zeros_like(db1_ref)
    dg_ref[...] = jnp.zeros_like(dg_ref)

    def backward_tile(i, carry):
        start = pl.multiple_of(i * TILE, TILE)
        rows = pl.ds(start, TILE)
        both = mm(dagg_ref[...], oht_ref[wide:, rows])
        cot = jnp.where(
            iota((TILE, feature), 0) + start < count, cot_ref[rows, :].astype(F32), 0.0
        )
        u = jnp.where(
            iota((feature, TILE), 1) + start < count, cot.T + (both[0:feature] + both[feature:]), 0.0
        )
        normed = normed_ref[:, rows]
        d_out_half = norm_backward(u, normed, inv_ref[:, rows], eg, 0).astype(BF16)
        dg_ref[...] += fold_lanes(u * normed)
        dw2_ref[...] += mm_nt(act_ref[:, rows], d_out_half)
        d_pre = mm(ew2, d_out_half) * slope_ref[:, rows]
        db1_ref[...] += fold_lanes(d_pre)
        d_pre_half = d_pre.astype(BF16)
        d_edges_ref[rows, :] = (cot + mm_tn(d_pre_half, ew1_edge_t)).astype(BF16)
        dw1_ref[...] += mm(d_pre_half, edges_ref[rows, :])
        s_ref[...] += mm_nt(oht_ref[:, rows], d_pre_half)
        return carry

    lax.fori_loop(0, tiles, backward_tile, 0, unroll=UNROLL)
    d_edges_copy = pltpu.make_async_copy(d_edges_ref, d_edges_out, out_sem.at[1])
    d_edges_copy.start()

    grads_ref[0:128, :] = dw1_ref[...].T
    grads_ref[384:512, :] = dw2_ref[...]
    grads_ref[896:897, :] = jnp.sum(db1_ref[...].T, axis=0, keepdims=True)
    grads_ref[897:898, :] = jnp.sum(dg_ref[...].T, axis=0, keepdims=True)
    grads_ref[900:, :] = jnp.zeros_like(grads_ref[900:, :])
    high, low = two_parts(s_ref[0:wide, :])
    table = table_ref[...]
    grads_ref[128:256, :] = mm_tn(table, high) + mm_tn(table, low)
    d_table = mm_nt(high, ew1_src) + mm_nt(low, ew1_src)
    high, low = two_parts(s_ref[wide:, :])
    grads_ref[256:384, :] = mm_tn(node, high) + mm_tn(node, low)
    d_node_ref[...] += d_table[0:cells, :] + (mm_nt(high, ew1_dst) + mm_nt(low, ew1_dst))
    kinds = [
        d_table[cells + 8 * peers * k : cells + 8 * peers * (k + 1), :].reshape(peers, 8, feature)
        for k in range(3)
    ]
    slab = slab_in_plane()
    slabs = send_ref.shape[0] // peers
    pad = [jnp.zeros((peers, HEAD - 8, feature), F32)]
    blank = jnp.zeros((peers, HEAD, feature), BF16)
    for y in range(slabs):
        send_ref[peers * y : peers * (y + 1), 0:HEAD, :] = blank
    onward = jnp.where(slab == 0, kinds[1], kinds[2])
    same = [kinds[0], onward, match_rows.reshape(peers, 16, feature)]
    send_ref[pl.ds(peers * slab, peers), 0:HEAD, :] = jnp.concatenate(same, axis=1).astype(BF16)

    @pl.when(slab > 0)
    def _():
        rows = jnp.concatenate([kinds[1]] + pad, axis=1).astype(BF16)
        send_ref[pl.ds(peers * (slab - 1), peers), 0:HEAD, :] = rows

    @pl.when(slab < slabs - 1)
    def _():
        rows = jnp.concatenate([kinds[2]] + pad, axis=1).astype(BF16)
        send_ref[pl.ds(peers * (slab + 1), peers), 0:HEAD, :] = rows

    share = GRAD_ROWS // (slabs * peers)
    grads = grads_ref[...].reshape(slabs * peers, share, feature)
    send_ref[:, HEAD:, :] = grads.astype(BF16)
    edges_copy.wait()
    d_edges_copy.wait()


def finish_kernel(
    recv_ref, passed_ref, d_node_ref, fresh_ref, intra_ref, bound_ref,
    pick_ref, first_ref, second_ref, d_out_ref, coarse_ref,
):
    peers = intra_ref.shape[0]
    slabs = recv_ref.shape[0] // peers
    cells, feature = d_node_ref.shape
    slab = slab_in_plane()
    same = recv_ref[pl.ds(peers * slab, peers), 0:HEAD, :]

    def gradients(block):
        return block.astype(F32)[:, 0:8, :].reshape(8 * peers, feature).astype(BF16)

    hot = onehot_rows(column_of(intra_ref[...]), cells)
    total = mm_tn(hot, gradients(same))
    passed = passed_ref[...]
    lower = jnp.maximum(slab - 1, 0)
    upper = jnp.minimum(slab + 1, slabs - 1)
    for k, near, edge in ((0, lower, slab == 0), (1, upper, slab == slabs - 1)):
        column = face_column(bound_ref[k : k + 1, :], pick_ref[k])
        direct = gradients(recv_ref[pl.ds(peers * near, peers), 0:HEAD, :])
        total = total + mm_tn(onehot_rows(column, cells), jnp.where(edge, passed, direct))
    d_out_ref[...] = d_node_ref[...] + total
    partners = same[:, 16:32, :].reshape(16 * peers, feature)
    coarse = coarse_ref.shape[0]
    cell_row = iota((cells, coarse), 0)
    near = onehot((first_ref[...] == cell_row) | (second_ref[...] == cell_row))
    far = onehot(second_ref[...] - cells == iota((16 * peers, coarse), 0))
    coarse_ref[...] = (0.5 * (mm_tn(near, fresh_ref[...]) + mm_tn(far, partners))).astype(BF16)


def unpack_kernel(recv_ref, w1_ref, w2_ref, nw1_ref, nw2_ref, b1_ref, g_ref, nb1_ref, ng_ref):
    start = 0
    for out_ref in (w1_ref, w2_ref, nw1_ref, nw2_ref):
        rows = out_ref.shape[0]
        out_ref[...] = recv_ref[start : start + rows, :].astype(F32)
        start += rows
    tail = recv_ref[start : start + 16, :].astype(F32)
    for k, out_ref in enumerate((b1_ref, g_ref, nb1_ref, ng_ref)):
        out_ref[...] = tail[k : k + 1, :]


def call(kernel, out_shape, *args, scratch=(), smem=(), hbm=(), hbm_out=(), name=None, cost=None, mib=8):
    def space(i, far):
        return pltpu.HBM if i in far else pltpu.VMEM

    one = not isinstance(out_shape, tuple)
    outs = [pl.BlockSpec(memory_space=space(i, hbm_out)) for i in range(1 if one else len(out_shape))]
    return pl.pallas_call(
        kernel,
        out_shape=out_shape,
        in_specs=[
            pl.BlockSpec(memory_space=pltpu.SMEM if i in smem else space(i, hbm)) for i in range(len(args))
        ],
        out_specs=outs[0] if one else tuple(outs),
        scratch_shapes=list(scratch),
        compiler_params=pltpu.CompilerParams(vmem_limit_bytes=mib * MIB),
        name=name,
        cost_estimate=cost,
    )(*args)


def shape_of(shape, dtype):
    return jax.ShapeDtypeStruct(shape, dtype)


def per_device(
    slabs, node, edges, edge_src, edge_dst, edge_count, intra_idx, bound_idx, cross_pick,
    match_send, pool_first, pool_second, edge_w1, edge_b1, edge_w2, edge_gain,
    node_w1, node_b1, node_w2, node_gain, edge_cot, coarse_cot,
):
    node, edges, edge_cot, coarse_cot = node[0, 0], edges[0, 0], edge_cot[0, 0], coarse_cot[0, 0]
    intra, bound, pick, match = intra_idx[0, 0], bound_idx[0, 0], cross_pick[0], match_send[0, 0]
    first, second = pool_first[0], pool_second[0]
    src, dst = edge_src[0], edge_dst[0]
    cells, feature = node.shape
    slots = edges.shape[0]
    coarse = coarse_cot.shape[0]
    peers = lax.axis_size("sub")
    planes = lax.axis_size("z")
    in_plane = slabs // planes
    dom = ("z", "y1", "y0")
    face = shape_of((8 * peers, feature), BF16)
    wide = -(-(cells + 24 * peers) // 256) * 256

    def swap(rows, step):
        pairs = [(i - 1, i) for i in range(step, slabs, step)]
        return lax.ppermute(rows, dom, pairs + [(j, i) for i, j in pairs])

    def exchange(blocks, axes):
        return lax.all_to_all(blocks, axes, split_axis=0, concat_axis=0, tiled=True)

    passed = swap(call(face_kernel, face, node, bound, pick, name="faces", mib=58), 2)
    sent = call(
        send_kernel, shape_of((2 * peers, HEAD, feature), BF16),
        node, intra, second, coarse_cot, bound, pick, name="send", mib=58,
        cost=pl.CostEstimate(flops=60_000_000, bytes_accessed=400_000, transcendentals=0),
    )
    sent = lax.dynamic_update_slice(
        sent, passed.reshape(peers, 8, feature), (peers * lax.axis_index("y0"), 8, 0)
    )
    received = exchange(sent, PAIR)

    far = (
        src, dst, node, edge_w1, edges, edge_b1[None], edge_w2, edge_gain[None],
        coarse_cot, first, second, match, node_w1, node_b1[None], node_w2, node_gain[None], edge_cot,
    )
    new_edges, d_edges, d_node, fresh, sent = call(
        main_kernel,
        (
            shape_of((slots, feature), BF16),
            shape_of((slots, feature), BF16),
            shape_of((cells, feature), F32),
            shape_of((cells, feature), BF16),
            shape_of((in_plane * peers, HEAD + GRAD_ROWS // (in_plane * peers), feature), BF16),
        ),
        edge_count, received, *far,
        smem=(0,),
        hbm=range(2, 2 + len(far)),
        hbm_out=(0, 1),
        scratch=[pltpu.VMEM(x.shape, x.dtype) for x in far]
        + [
            pltpu.VMEM((slots, feature), BF16),
            pltpu.VMEM((slots, feature), BF16),
            pltpu.VMEM((wide, feature), BF16),
            pltpu.VMEM((2 * feature, wide + cells), BF16),
            pltpu.VMEM((wide + cells, slots), BF16),
            pltpu.VMEM((cells, 2 * feature), F32),
            pltpu.VMEM((feature, slots), BF16),
            pltpu.VMEM((feature, slots), F32),
            pltpu.VMEM((feature, slots), F32),
            pltpu.VMEM((1, slots), F32),
            pltpu.VMEM((2 * feature, cells), BF16),
            pltpu.VMEM((wide + cells, feature), F32),
            pltpu.VMEM((feature, feature), F32),
            pltpu.VMEM((feature, feature), F32),
            pltpu.VMEM((feature, feature), F32),
            pltpu.VMEM((feature, feature), F32),
            pltpu.VMEM((GRAD_ROWS, feature), F32),
            pltpu.SemaphoreType.DMA((len(far),)),
            pltpu.SemaphoreType.DMA((2,)),
        ],
        name="layer",
        mib=58,
    )
    received = exchange(sent, PLANE)
    onward = lax.dynamic_slice(received, (peers * slab_in_plane(), 8, 0), (peers, 8, feature))
    passed = swap(onward.reshape(8 * peers, feature), in_plane)
    scale = 1.0 / math.sqrt(slabs * peers * slots)

    def total(blocks, factor, copies):
        rows = (jnp.sum(blocks.astype(F32), axis=0) * factor).astype(BF16)
        return jnp.broadcast_to(rows, (copies,) + rows.shape)

    summed = exchange(total(received[:, HEAD:], 1.0, planes), "z")
    grads = exchange(total(summed, scale, in_plane * peers), PLANE)
    d_node, coarse_out = call(
        finish_kernel,
        (shape_of((cells, feature), F32), shape_of((coarse, feature), BF16)),
        received, passed, d_node, fresh, intra, bound, pick, first, second,
        name="finish",
        cost=pl.CostEstimate(flops=300_000_000, bytes_accessed=2_000_000, transcendentals=0),
    )
    row = shape_of((1, feature), F32)
    w1, w2, nw1, nw2, b1, g, nb1, ng = call(
        unpack_kernel,
        (
            shape_of((3 * feature, feature), F32),
            shape_of((feature, feature), F32),
            shape_of((2 * feature, feature), F32),
            shape_of((feature, feature), F32),
            row, row, row, row,
        ),
        grads.reshape(GRAD_ROWS, feature),
        name="unpack",
    )
    return (
        new_edges[None, None], coarse_out[None, None], d_node[None, None], d_edges[None, None],
        w1, b1[0], w2, g[0], nw1, nb1[0], nw2, ng[0],
    )


def solution(mesh):
    slabs, peers = mesh.shape["dom"], mesh.shape["sub"]
    devices = mesh.devices.reshape(slabs // 4, 2, 2, peers)
    dom = ("z", "y1", "y0")
    inner = Mesh(devices, dom + ("sub",))
    four, three = P(dom, "sub", None, None), P(dom, "sub", None)
    return jax.shard_map(
        functools.partial(per_device, slabs),
        mesh=inner,
        in_specs=(
            four, four, three, three, P(dom, "sub"), four, four, P("sub", None, None, None),
            four, three, three, P(), P(), P(), P(), P(), P(), P(), P(), four, four,
        ),
        out_specs=(four, four, four, four) + (P(),) * 8,
        check_vma=False,
    )
```

```python
import functools
import math

import jax
import jax.numpy as jnp
from jax import lax
from jax.experimental import pallas as pl
from jax.experimental.pallas import tpu as pltpu
from jax.sharding import Mesh
from jax.sharding import PartitionSpec as P

NORM_EPSILON = 1e-05
F32 = jnp.float32
BF16 = jnp.bfloat16
MIB = 1024 * 1024

PAIR = ("y0", "sub")
PLANE = ("y1", "y0", "sub")
FIRST = 32
HEAD = 24
GRAD_ROWS = 1024


def mm(a, b):
    return lax.dot_general(a, b, (((1,), (0,)), ((), ())), preferred_element_type=F32)


def mm_nt(a, b):
    return lax.dot_general(a, b, (((1,), (1,)), ((), ())), preferred_element_type=F32)


def mm_tn(a, b):
    return lax.dot_general(a, b, (((0,), (0,)), ((), ())), preferred_element_type=F32)


def iota(shape, dim):
    return lax.broadcasted_iota(jnp.int32, shape, dim)


def onehot(mask):
    return jnp.where(mask, 1.0, 0.0).astype(BF16)


def two_parts(x):
    high = x.astype(BF16)
    low = (x - high.astype(F32)).astype(BF16)
    return high, low


def column_of(ids):
    a, b = ids.shape
    spread = jnp.broadcast_to(ids[:, None, :], (a, b, b))
    keep = iota((a, b, b), 1) == iota((a, b, b), 2)
    return jnp.sum(jnp.where(keep, spread, 0), axis=2, keepdims=True).reshape(a * b, 1)


def face_column(face_row, pick):
    spot = column_of(pick)
    shape = (spot.shape[0], face_row.shape[1])
    keep = spot == iota(shape, 1)
    return jnp.sum(jnp.where(keep, jnp.broadcast_to(face_row, shape), 0), axis=1, keepdims=True)


def onehot_rows(column, width):
    return onehot(column == iota((column.shape[0], width), 1))


def slab_in_plane():
    return lax.axis_index("y1") * lax.axis_size("y0") + lax.axis_index("y0")


def picked_rows(node, bound_ref, pick_ref, side):
    face_row = jnp.where(side == 0, bound_ref[0:1, :], bound_ref[1:2, :])
    return mm(onehot_rows(face_column(face_row, pick_ref[side]), node.shape[0]), node)


def face_kernel(node_ref, bound_ref, pick_ref, out_ref):
    out_ref[...] = picked_rows(node_ref[...], bound_ref, pick_ref, lax.axis_index("y0")).astype(BF16)


def send_kernel(count_ref, intra_ref, bound_ref, pick_ref, *refs):
    arrays = (len(refs) - 4) // 2
    far, near, sem = refs[:arrays], refs[arrays + 3 : -1], refs[-1]
    out_ref, count_out_ref, onward_ref = refs[arrays : arrays + 3]
    copies = [pltpu.make_async_copy(far[k], near[k], sem.at[k]) for k in range(arrays)]
    for copy in copies:
        copy.start()
    node_ref, second_ref, coarse_cot_ref = near[0:3]
    count_out_ref[...] = jnp.full(count_out_ref.shape, count_ref[0, 0], jnp.int32)
    slab = slab_in_plane()
    last = lax.axis_size("y1") * lax.axis_size("y0") - 1
    half_rows = onward_ref.shape[0] // 2
    for k, reader in ((0, last), (1, 0)):
        column = jnp.where(slab == reader, column_of(pick_ref[1 - k]), -1)
        onward_ref[half_rows * k : half_rows * (k + 1), :] = onehot_rows(column, 128)
    for copy in copies[0:3]:
        copy.wait()
    odd = lax.axis_index("y0")
    node = node_ref[...]
    cells, feature = node.shape
    peers, halo = intra_ref.shape
    coarse = coarse_cot_ref.shape[0]
    intra = mm(onehot_rows(column_of(intra_ref[...]), cells), node)
    half = 0.5 * coarse_cot_ref[...].astype(F32)
    pool_rows = 16 * peers
    pool = mm(onehot(second_ref[...] - cells == iota((pool_rows, coarse), 0)), half.astype(BF16))
    same = [
        intra.reshape(peers, halo, feature),
        jnp.zeros((peers, halo, feature), F32),
        pool.reshape(peers, 16, feature),
    ]
    other = [
        picked_rows(node, bound_ref, pick_ref, 1 - odd).reshape(peers, halo, feature),
        jnp.zeros((peers, FIRST - halo, feature), F32),
    ]
    out_ref[pl.ds(peers * odd, peers)] = jnp.concatenate(same, axis=1).astype(BF16)
    out_ref[pl.ds(peers * (1 - odd), peers)] = jnp.concatenate(other, axis=1).astype(BF16)
    for copy in copies[3:]:
        copy.wait()


def silu_parts(pre):
    sig = 0.5 * jnp.tanh(0.5 * pre) + 0.5
    act = (pre * sig).astype(BF16)
    slope = sig * (1.0 + pre * (1.0 - sig))
    return act, slope


def norm_forward(out, axis):
    centred = out - jnp.mean(out, axis=axis, keepdims=True)
    inv = lax.rsqrt(jnp.mean(centred * centred, axis=axis, keepdims=True) + NORM_EPSILON)
    return centred * inv, inv


def norm_backward(u, normed, inv, gain, axis):
    scaled = u * gain
    inner = (
        scaled
        - jnp.mean(scaled, axis=axis, keepdims=True)
        - normed * jnp.mean(scaled * normed, axis=axis, keepdims=True)
    )
    return inner * inv


def fold_lanes(x):
    total = x[:, 0:128]
    for k in range(1, x.shape[1] // 128):
        total = total + x[:, 128 * k : 128 * k + 128]
    return total


def column_block(row, width):
    block = jnp.broadcast_to(row, (128, 128)).T
    return jnp.concatenate([block] * (width // 128), axis=1)


def hot_columns(ids, rows):
    width = ids.shape[1]

    def spread(x):
        return jnp.broadcast_to(x.astype(F32), (16, width)).astype(BF16)

    tens, units = spread(ids & -16), spread(ids & 15)
    zero = jnp.zeros((16, width), BF16)
    base = jnp.where(units == iota((16, width), 0).astype(F32).astype(BF16), jnp.ones((16, width), BF16), zero)
    return jnp.concatenate(
        [jnp.where(tens == jnp.full((16, width), 16 * r, BF16), base, zero) for r in range(rows // 16)], axis=0
    )


def main_kernel(
    count_ref, recv_ref, node_ref, second_ref, coarse_cot_ref, src_ref, dst_ref, ew1_ref, eb1_ref, edges_ref,
    ew2_ref, eg_ref, nw1_ref, nb1_ref, nw2_ref, ng_ref, first_ref, match_ref, cot_ref,
    new_edges_out, d_edges_out, d_node_ref, fresh_ref, send_ref,
    new_edges_ref, d_edges_ref, table_ref, t2_ref, oht_ref, grads_ref, out_sem,
):
    cells, feature = node_ref.shape
    wide = table_ref.shape[0]
    oht_ref[0:wide, :] = hot_columns(src_ref[...], wide)
    oht_ref[wide:, :] = hot_columns(dst_ref[...], cells)
    slots = edges_ref.shape[0]
    peers = recv_ref.shape[0] // 2
    count = count_ref[0:1, 0:1]
    node = node_ref[...]
    odd = lax.axis_index("y0")
    same = recv_ref[pl.ds(peers * odd, peers)]
    near = same.astype(F32)
    other = recv_ref[pl.ds(peers * (1 - odd), peers)].astype(F32)[:, 0:8, :]
    passed = near[:, 8:16, :]
    kinds = [near[:, 0:8, :], jnp.where(odd == 0, passed, other), jnp.where(odd == 0, other, passed)]
    halo_rows = 3 * 8 * peers
    table_ref[0:cells, :] = node
    halo = jnp.concatenate(
        [rows.reshape(8 * peers, feature) for rows in kinds]
        + [jnp.zeros((wide - cells - halo_rows, feature), F32)],
        axis=0,
    )
    table_ref[cells:wide, :] = halo.astype(BF16)
    ew1_edge_t = ew1_ref[0:feature, :].T
    ew1_src = ew1_ref[feature : 2 * feature, :]
    ew1_dst = ew1_ref[2 * feature : 3 * feature, :]
    high, low = two_parts(mm_nt(ew1_src.T, table_ref[...]))
    t2_ref[0:feature, 0:wide] = high
    t2_ref[feature:, 0:wide] = low
    high, low = two_parts(mm_nt(ew1_dst.T, node) + column_block(eb1_ref[...], cells))
    t2_ref[0:feature, wide:] = high
    t2_ref[feature:, wide:] = low
    ew2 = ew2_ref[...]
    eg = column_block(eg_ref[...], slots)
    live_column = iota((feature, slots), 1) < count
    live_row = iota((slots, feature), 0) < count

    both = mm(t2_ref[...], oht_ref[...])
    pre = both[0:feature] + both[feature:] + mm_nt(ew1_edge_t, edges_ref[...])
    edge_act, edge_slope = silu_parts(pre)
    edge_normed, edge_inv = norm_forward(mm(ew2.T, edge_act), 0)
    message = jnp.where(live_column, edge_normed * eg, 0.0)
    new_edges = jnp.where(live_row, edges_ref[...].astype(F32) + message.T, 0.0)
    new_edges_ref[...] = new_edges.astype(BF16)
    edges_copy = pltpu.make_async_copy(new_edges_ref, new_edges_out, out_sem.at[0])
    edges_copy.start()
    both = mm_nt(oht_ref[wide:, :], jnp.concatenate(two_parts(message), axis=0))
    aggregate = (both[:, 0:feature] + both[:, feature:]).astype(BF16)

    nw1_node = nw1_ref[0:feature, :]
    nw1_agg = nw1_ref[feature:, :]
    pre = mm(node, nw1_node) + mm(aggregate, nw1_agg) + nb1_ref[...]
    act, slope = silu_parts(pre)
    nw2 = nw2_ref[...]
    ng = ng_ref[...]
    normed, inv = norm_forward(mm(act, nw2), 1)
    fresh = (node.astype(F32) + normed * ng).astype(BF16)
    fresh_ref[...] = fresh

    coarse = coarse_cot_ref.shape[0]
    half = (0.5 * coarse_cot_ref[...].astype(F32)).astype(BF16)
    cell_row = iota((cells, coarse), 0)
    pooled = onehot((first_ref[...] == cell_row) | (second_ref[...] == cell_row))
    returned = same[:, 16:32, :].reshape(16 * peers, feature)
    hot_match = onehot_rows(column_of(match_ref[...]), cells)
    d_fresh = mm(pooled, half) + mm_tn(hot_match, returned)
    match_rows = mm(hot_match, fresh)

    d_out = norm_backward(d_fresh, normed, inv, ng, 1)
    grads_ref[899:900, :] = jnp.sum(d_fresh * normed, axis=0, keepdims=True)
    d_out_half = d_out.astype(BF16)
    grads_ref[768:896, :] = mm_tn(act, d_out_half)
    d_pre = mm_nt(d_out_half, nw2) * slope
    grads_ref[898:899, :] = jnp.sum(d_pre, axis=0, keepdims=True)
    d_pre_half = d_pre.astype(BF16)
    grads_ref[512:640, :] = mm_tn(node, d_pre_half)
    grads_ref[640:768, :] = mm_tn(aggregate, d_pre_half)
    d_node_ref[...] = d_fresh + mm_nt(d_pre_half, nw1_node)
    high, low = two_parts(mm_nt(nw1_agg, d_pre_half))

    both = mm(jnp.concatenate([high, low], axis=0), oht_ref[wide:, :])
    cot = jnp.where(live_row, cot_ref[...].astype(F32), 0.0)
    u = jnp.where(live_column, cot.T + (both[0:feature] + both[feature:]), 0.0)
    d_out_half = norm_backward(u, edge_normed, edge_inv, eg, 0).astype(BF16)
    d_gain = fold_lanes(u * edge_normed)
    d_pre = mm(ew2, d_out_half) * edge_slope
    d_pre_half = d_pre.astype(BF16)
    d_edges_ref[...] = (cot + mm_tn(d_pre_half, ew1_edge_t)).astype(BF16)
    d_edges_copy = pltpu.make_async_copy(d_edges_ref, d_edges_out, out_sem.at[1])
    d_edges_copy.start()
    scattered = mm_nt(oht_ref[...], d_pre_half)

    grads_ref[0:128, :] = mm(d_pre_half, edges_ref[...]).T
    grads_ref[384:512, :] = mm_nt(edge_act, d_out_half)
    grads_ref[896:897, :] = jnp.sum(fold_lanes(d_pre).T, axis=0, keepdims=True)
    grads_ref[897:898, :] = jnp.sum(d_gain.T, axis=0, keepdims=True)
    grads_ref[900:, :] = jnp.zeros_like(grads_ref[900:, :])
    high, low = two_parts(scattered[0:wide])
    table = table_ref[...]
    grads_ref[128:256, :] = mm_tn(table, high) + mm_tn(table, low)
    d_table = mm_nt(high, ew1_src) + mm_nt(low, ew1_src)
    high, low = two_parts(scattered[wide:])
    grads_ref[256:384, :] = mm_tn(node, high) + mm_tn(node, low)
    d_node_ref[...] += d_table[0:cells, :] + (mm_nt(high, ew1_dst) + mm_nt(low, ew1_dst))
    kinds = [
        d_table[cells + 8 * peers * k : cells + 8 * peers * (k + 1), :].reshape(peers, 8, feature)
        for k in range(3)
    ]
    slab = slab_in_plane()
    slabs = send_ref.shape[0] // peers
    share = GRAD_ROWS // (slabs * peers)
    blank = jnp.zeros((peers, 8, feature), F32)
    first_plane, last_plane = slab == 0, slab == slabs - 1
    heads = [
        [kinds[0], match_rows.reshape(peers, 16, feature)],
        [kinds[2], jnp.where(last_plane, kinds[2], 0.0), blank],
    ]
    heads += [[blank, blank, blank]] * (slabs - 3)
    heads += [[kinds[1], jnp.where(first_plane, kinds[1], 0.0), blank]]
    for step, head in enumerate(heads):
        to = lax.rem(slab + step, slabs)
        grads = grads_ref[pl.ds(pl.multiple_of(to * (peers * share), 8), peers * share), :]
        block = jnp.concatenate(head + [grads.reshape(peers, share, feature)], axis=1)
        send_ref[pl.ds(peers * to, peers)] = block.astype(BF16)
    edges_copy.wait()
    d_edges_copy.wait()


def unpack(recv_ref, w1_ref, w2_ref, nw1_ref, nw2_ref, b1_ref, g_ref, nb1_ref, ng_ref):
    start = 0
    for out_ref in (w1_ref, w2_ref, nw1_ref, nw2_ref):
        rows = out_ref.shape[0]
        out_ref[...] = recv_ref[start : start + rows, :].astype(F32)
        start += rows
    tail = recv_ref[start : start + 16, :].astype(F32)
    for k, out_ref in enumerate((b1_ref, g_ref, nb1_ref, ng_ref)):
        out_ref[...] = tail[k : k + 1, :]


def finish_kernel(
    recv_ref, planes_ref, d_node_ref, fresh_ref, intra_ref, bound_ref,
    pick_ref, first_ref, second_ref, grads_ref, d_out_ref, coarse_ref, *weight_refs,
):
    unpack(grads_ref, *weight_refs)
    peers = intra_ref.shape[0]
    slabs = recv_ref.shape[0] // peers
    planes = planes_ref.shape[0]
    cells, feature = d_node_ref.shape
    slab = slab_in_plane()
    plane = lax.axis_index("z")

    def block_of(y):
        return recv_ref[pl.ds(peers * y, peers)].astype(F32)

    def gradients(block):
        return block[:, 0:8, :].reshape(8 * peers, feature).astype(BF16)

    same = block_of(slab)
    hot = onehot_rows(column_of(intra_ref[...]), cells)
    total = mm_tn(hot, gradients(same))
    faces = bound_ref.shape[1]
    first_row = planes_ref.shape[1] - faces
    for k, step, edge in ((0, -1, slab == 0), (1, 1, slab == slabs - 1)):
        face_row = bound_ref[k : k + 1, :]
        direct = gradients(block_of(lax.rem(slab + step + slabs, slabs)))
        direct = jnp.where(edge, jnp.zeros_like(direct), direct)
        total = total + mm_tn(onehot_rows(face_column(face_row, pick_ref[k]), cells), direct)
        far = jnp.clip(plane + step, 0, planes - 1)
        passed = planes_ref[far, first_row:, :]
        passed = jnp.where(edge & (far != plane), passed, jnp.zeros_like(passed))
        total = total + mm_tn(onehot_rows(column_of(face_row), cells), passed)
    d_out_ref[...] = d_node_ref[...] + total
    partners = same[:, 8:24, :].reshape(16 * peers, feature).astype(BF16)
    coarse = coarse_ref.shape[0]
    cell_row = iota((cells, coarse), 0)
    near = onehot((first_ref[...] == cell_row) | (second_ref[...] == cell_row))
    far = onehot(second_ref[...] - cells == iota((16 * peers, coarse), 0))
    coarse_ref[...] = (0.5 * (mm_tn(near, fresh_ref[...]) + mm_tn(far, partners))).astype(BF16)


def call(kernel, out_shape, *args, scratch=(), smem=(), hbm=(), hbm_out=(), held=(), name=None, cost=None, mib=8):
    def space(i, far):
        return pltpu.HBM if i in far else pltpu.VMEM

    one = not isinstance(out_shape, tuple)
    outs = [pl.BlockSpec(memory_space=space(i, hbm_out)) for i in range(1 if one else len(out_shape))]
    args = [pltpu.with_memory_space_constraint(x, pltpu.HBM) if i in hbm or i in held else x for i, x in enumerate(args)]
    return pl.pallas_call(
        kernel,
        out_shape=out_shape,
        in_specs=[
            pl.BlockSpec(memory_space=pltpu.SMEM if i in smem else space(i, hbm)) for i in range(len(args))
        ],
        out_specs=outs[0] if one else tuple(outs),
        scratch_shapes=list(scratch),
        compiler_params=pltpu.CompilerParams(vmem_limit_bytes=mib * MIB),
        name=name,
        cost_estimate=cost,
    )(*args)


def shape_of(shape, dtype):
    return jax.ShapeDtypeStruct(shape, dtype)


def per_device(
    slabs, node, edges, edge_src, edge_dst, edge_count, intra_idx, bound_idx, cross_pick,
    match_send, pool_first, pool_second, edge_w1, edge_b1, edge_w2, edge_gain,
    node_w1, node_b1, node_w2, node_gain, edge_cot, coarse_cot,
):
    node, edges, edge_cot, coarse_cot = node[0, 0], edges[0, 0], edge_cot[0, 0], coarse_cot[0, 0]
    intra, bound, pick, match = intra_idx[0, 0], bound_idx[0, 0], cross_pick[0], match_send[0, 0]
    first, second = pool_first[0], pool_second[0]
    src, dst = edge_src[0], edge_dst[0]
    cells, feature = node.shape
    slots = edges.shape[0]
    coarse = coarse_cot.shape[0]
    peers = lax.axis_size("sub")
    planes = lax.axis_size("z")
    in_plane = slabs // planes
    dom = ("z", "y1", "y0")
    face = shape_of((8 * peers, feature), BF16)
    wide = -(-(cells + 24 * peers) // 256) * 256

    def swap(rows):
        pairs = [(i - 1, i) for i in range(2, slabs, 2)]
        return lax.ppermute(rows, dom, pairs + [(j, i) for i, j in pairs])

    def exchange(blocks, axes):
        return lax.all_to_all(blocks, axes, split_axis=0, concat_axis=0, tiled=True)

    passed = swap(call(face_kernel, face, node, bound, pick, held=range(3), name="faces"))
    far = (
        node, second, coarse_cot, src, dst, edge_w1, edge_b1[None], edges, edge_w2, edge_gain[None],
        node_w1, node_b1[None], node_w2, node_gain[None], first, match, edge_cot, intra, bound, pick,
    )
    sent, count, onward_pick, *near = call(
        send_kernel,
        (shape_of((2 * peers, FIRST, feature), BF16), shape_of((8, 128), jnp.int32), shape_of((16 * peers, 128), BF16))
        + tuple(shape_of(x.shape, x.dtype) for x in far),
        edge_count, intra, bound, pick, *far,
        smem=(0,), held=range(1, 4), hbm=range(4, 4 + len(far)),
        scratch=[pltpu.SemaphoreType.DMA((len(far),))],
        name="send",
        cost=pl.CostEstimate(flops=60_000_000, bytes_accessed=400_000, transcendentals=0),
    )
    passed = passed.reshape(peers, 8, feature)
    passed = jnp.concatenate([passed, passed], axis=0)
    sent = jnp.concatenate([sent[:, 0:8], passed, sent[:, 16:]], axis=1)
    received = exchange(sent, PAIR)

    new_edges, d_edges, d_node, fresh, sent = call(
        main_kernel,
        (
            shape_of((slots, feature), BF16),
            shape_of((slots, feature), BF16),
            shape_of((cells, feature), F32),
            shape_of((cells, feature), BF16),
            shape_of((in_plane * peers, HEAD + GRAD_ROWS // (in_plane * peers), feature), BF16),
        ),
        count, received, *near[:-3],
        hbm_out=(0, 1),
        scratch=[
            pltpu.VMEM((slots, feature), BF16),
            pltpu.VMEM((slots, feature), BF16),
            pltpu.VMEM((wide, feature), BF16),
            pltpu.VMEM((2 * feature, wide + cells), BF16),
            pltpu.VMEM((wide + cells, slots), BF16),
            pltpu.VMEM((GRAD_ROWS, feature), F32),
            pltpu.SemaphoreType.DMA((2,)),
        ],
        name="layer",
        mib=28,
    )
    received = exchange(sent, PLANE)
    scale = 1.0 / math.sqrt(slabs * peers * slots)

    def total(blocks):
        return jnp.sum(blocks.astype(F32), axis=0)

    def copies(rows, count):
        return jnp.broadcast_to(rows, (count,) + rows.shape)

    ends = jnp.concatenate([received[0:peers, 8:16], received[-peers:, 8:16]], axis=0)
    onward = mm_tn(onward_pick, ends.reshape(16 * peers, feature))[0 : bound.shape[1]]
    rows = jnp.concatenate([total(received[:, HEAD:]), onward], axis=0).astype(BF16)
    by_plane = exchange(copies(rows, planes), "z")
    share = rows.shape[0] - onward.shape[0]
    rows = (total(by_plane[:, 0:share]) * scale).astype(BF16)
    grads = exchange(copies(rows, in_plane * peers), PLANE)
    row = shape_of((1, feature), F32)
    d_node, coarse_out, w1, w2, nw1, nw2, b1, g, nb1, ng = call(
        finish_kernel,
        (
            shape_of((cells, feature), F32),
            shape_of((coarse, feature), BF16),
            shape_of((3 * feature, feature), F32),
            shape_of((feature, feature), F32),
            shape_of((2 * feature, feature), F32),
            shape_of((feature, feature), F32),
            row, row, row, row,
        ),
        received, by_plane, d_node, fresh, *near[-3:], near[14], near[1], grads.reshape(GRAD_ROWS, feature),
        name="finish",
    )
    return (
        new_edges[None, None], coarse_out[None, None], d_node[None, None], d_edges[None, None],
        w1, b1[0], w2, g[0], nw1, nb1[0], nw2, ng[0],
    )


def solution(mesh):
    slabs, peers = mesh.shape["dom"], mesh.shape["sub"]
    devices = mesh.devices.reshape(slabs // 4, 2, 2, peers)
    dom = ("z", "y1", "y0")
    inner = Mesh(devices, dom + ("sub",))
    four, three = P(dom, "sub", None, None), P(dom, "sub", None)
    return jax.shard_map(
        functools.partial(per_device, slabs),
        mesh=inner,
        in_specs=(
            four, four, three, three, P(dom, "sub"), four, four, P("sub", None, None, None),
            four, three, three, P(), P(), P(), P(), P(), P(), P(), P(), four, four,
        ),
        out_specs=(four, four, four, four) + (P(),) * 8,
        check_vma=False,
    )
```

```python
import functools
import math

import jax
import jax.numpy as jnp
from jax import lax
from jax.experimental import pallas as pl
from jax.experimental.pallas import tpu as pltpu
from jax.sharding import Mesh
from jax.sharding import PartitionSpec as P

NORM_EPSILON = 1e-05
F32 = jnp.float32
BF16 = jnp.bfloat16
MIB = 1024 * 1024

PAIR = ("y0", "sub")
PLANE = ("y1", "y0", "sub")
FIRST = 32
HEAD = 24
GRAD_ROWS = 1024


def mm(a, b):
    return lax.dot_general(a, b, (((1,), (0,)), ((), ())), preferred_element_type=F32)


def mm_nt(a, b):
    return lax.dot_general(a, b, (((1,), (1,)), ((), ())), preferred_element_type=F32)


def mm_tn(a, b):
    return lax.dot_general(a, b, (((0,), (0,)), ((), ())), preferred_element_type=F32)


def iota(shape, dim):
    return lax.broadcasted_iota(jnp.int32, shape, dim)


def onehot(mask):
    return jnp.where(mask, 1.0, 0.0).astype(BF16)


def two_parts(x):
    high = x.astype(BF16)
    low = (x - high.astype(F32)).astype(BF16)
    return high, low


def column_of(ids):
    a, b = ids.shape
    spread = jnp.broadcast_to(ids[:, None, :], (a, b, b))
    keep = iota((a, b, b), 1) == iota((a, b, b), 2)
    return jnp.sum(jnp.where(keep, spread, 0), axis=2, keepdims=True).reshape(a * b, 1)


def face_column(face_row, pick):
    spot = column_of(pick)
    shape = (spot.shape[0], face_row.shape[1])
    keep = spot == iota(shape, 1)
    return jnp.sum(jnp.where(keep, jnp.broadcast_to(face_row, shape), 0), axis=1, keepdims=True)


def onehot_rows(column, width):
    return onehot(column == iota((column.shape[0], width), 1))


def slab_in_plane():
    return lax.axis_index("y1") * lax.axis_size("y0") + lax.axis_index("y0")


def picked_rows(node, bound_ref, pick_ref, side):
    face_row = jnp.where(side == 0, bound_ref[0:1, :], bound_ref[1:2, :])
    return mm(onehot_rows(face_column(face_row, pick_ref[side]), node.shape[0]), node)


def face_kernel(node_ref, bound_ref, pick_ref, out_ref):
    out_ref[...] = picked_rows(node_ref[...], bound_ref, pick_ref, lax.axis_index("y0")).astype(BF16)


def send_kernel(count_ref, intra_ref, bound_ref, pick_ref, *refs):
    arrays = (len(refs) - 4) // 2
    far, near, sem = refs[:arrays], refs[arrays + 3 : -1], refs[-1]
    out_ref, count_out_ref, onward_ref = refs[arrays : arrays + 3]
    copies = [pltpu.make_async_copy(far[k], near[k], sem.at[k]) for k in range(arrays)]
    for copy in copies:
        copy.start()
    node_ref, second_ref, coarse_cot_ref = near[0:3]
    count_out_ref[...] = jnp.full(count_out_ref.shape, count_ref[0, 0], jnp.int32)
    slab = slab_in_plane()
    last = lax.axis_size("y1") * lax.axis_size("y0") - 1
    half_rows = onward_ref.shape[0] // 2
    for k, reader in ((0, last), (1, 0)):
        column = jnp.where(slab == reader, column_of(pick_ref[1 - k]), -1)
        onward_ref[half_rows * k : half_rows * (k + 1), :] = onehot_rows(column, 128)
    for copy in copies[0:3]:
        copy.wait()
    odd = lax.axis_index("y0")
    node = node_ref[...]
    cells, feature = node.shape
    peers, halo = intra_ref.shape
    coarse = coarse_cot_ref.shape[0]
    intra = mm(onehot_rows(column_of(intra_ref[...]), cells), node)
    half = 0.5 * coarse_cot_ref[...].astype(F32)
    pool_rows = 16 * peers
    pool = mm(onehot(second_ref[...] - cells == iota((pool_rows, coarse), 0)), half.astype(BF16))
    same = [
        intra.reshape(peers, halo, feature),
        jnp.zeros((peers, halo, feature), F32),
        pool.reshape(peers, 16, feature),
    ]
    other = [
        picked_rows(node, bound_ref, pick_ref, 1 - odd).reshape(peers, halo, feature),
        jnp.zeros((peers, FIRST - halo, feature), F32),
    ]
    out_ref[pl.ds(peers * odd, peers)] = jnp.concatenate(same, axis=1).astype(BF16)
    out_ref[pl.ds(peers * (1 - odd), peers)] = jnp.concatenate(other, axis=1).astype(BF16)
    for copy in copies[3:]:
        copy.wait()


def silu_parts(pre):
    sig = 0.5 * jnp.tanh(0.5 * pre) + 0.5
    act = (pre * sig).astype(BF16)
    slope = sig * (1.0 + pre * (1.0 - sig))
    return act, slope


def norm_forward(out, axis):
    centred = out - jnp.mean(out, axis=axis, keepdims=True)
    inv = lax.rsqrt(jnp.mean(centred * centred, axis=axis, keepdims=True) + NORM_EPSILON)
    return centred * inv, inv


def norm_backward(u, normed, inv, gain, axis):
    scaled = u * gain
    inner = (
        scaled
        - jnp.mean(scaled, axis=axis, keepdims=True)
        - normed * jnp.mean(scaled * normed, axis=axis, keepdims=True)
    )
    return inner * inv


def fold_lanes(x):
    total = x[:, 0:128]
    for k in range(1, x.shape[1] // 128):
        total = total + x[:, 128 * k : 128 * k + 128]
    return total


def column_block(row, width):
    block = jnp.broadcast_to(row, (128, 128)).T
    return jnp.concatenate([block] * (width // 128), axis=1)


def hot_columns(ids, rows):
    width = ids.shape[1]

    def spread(x):
        return jnp.broadcast_to(x.astype(F32), (16, width)).astype(BF16)

    tens, units = spread(ids & -16), spread(ids & 15)
    zero = jnp.zeros((16, width), BF16)
    base = jnp.where(units == iota((16, width), 0).astype(F32).astype(BF16), jnp.ones((16, width), BF16), zero)
    return jnp.concatenate(
        [jnp.where(tens == jnp.full((16, width), 16 * r, BF16), base, zero) for r in range(rows // 16)], axis=0
    )


def main_kernel(
    count_ref, recv_ref, node_ref, second_ref, coarse_cot_ref, src_ref, dst_ref, ew1_ref, eb1_ref, edges_ref,
    ew2_ref, eg_ref, nw1_ref, nb1_ref, nw2_ref, ng_ref, first_ref, match_ref, cot_ref,
    new_edges_out, d_edges_out, d_node_ref, fresh_ref, send_ref,
    new_edges_ref, d_edges_ref, table_ref, ends_ref, oht_ref, grads_ref, out_sem,
):
    cells, feature = node_ref.shape
    wide = table_ref.shape[0]
    oht_ref[0:wide, :] = hot_columns(src_ref[...], wide)
    oht_ref[wide:, :] = hot_columns(dst_ref[...], cells)
    slots = edges_ref.shape[0]
    peers = recv_ref.shape[0] // 2
    count = count_ref[0:1, 0:1]
    node = node_ref[...]
    odd = lax.axis_index("y0")
    same = recv_ref[pl.ds(peers * odd, peers)]
    near = same.astype(F32)
    other = recv_ref[pl.ds(peers * (1 - odd), peers)].astype(F32)[:, 0:8, :]
    passed = near[:, 8:16, :]
    kinds = [near[:, 0:8, :], jnp.where(odd == 0, passed, other), jnp.where(odd == 0, other, passed)]
    halo_rows = 3 * 8 * peers
    table_ref[0:cells, :] = node
    halo = jnp.concatenate(
        [rows.reshape(8 * peers, feature) for rows in kinds]
        + [jnp.zeros((wide - cells - halo_rows, feature), F32)],
        axis=0,
    )
    table_ref[cells:wide, :] = halo.astype(BF16)
    ew1_edge_t = ew1_ref[0:feature, :].T
    ew1_src = ew1_ref[feature : 2 * feature, :]
    ew1_dst = ew1_ref[2 * feature : 3 * feature, :]
    ew2 = ew2_ref[...]
    eg = column_block(eg_ref[...], slots)
    live_column = iota((feature, slots), 1) < count
    live_row = iota((slots, feature), 0) < count

    ends_ref[0:feature, :] = mm(table_ref[...].T, oht_ref[0:wide, :]).astype(BF16)
    ends_ref[feature:, :] = mm(node.T, oht_ref[wide:, :]).astype(BF16)
    pre = mm(ew1_ref[feature:, :].T, ends_ref[...]) + mm_nt(ew1_edge_t, edges_ref[...])
    pre = pre + column_block(eb1_ref[...], slots)
    edge_act, edge_slope = silu_parts(pre)
    edge_normed, edge_inv = norm_forward(mm(ew2.T, edge_act), 0)
    message = jnp.where(live_column, edge_normed * eg, 0.0)
    new_edges = jnp.where(live_row, edges_ref[...].astype(F32) + message.T, 0.0)
    new_edges_ref[...] = new_edges.astype(BF16)
    edges_copy = pltpu.make_async_copy(new_edges_ref, new_edges_out, out_sem.at[0])
    edges_copy.start()
    both = mm_nt(jnp.concatenate(two_parts(message), axis=0), oht_ref[wide:, :])
    aggregate = (both[0:feature] + both[feature:]).T.astype(BF16)

    nw1_node = nw1_ref[0:feature, :]
    nw1_agg = nw1_ref[feature:, :]
    pre = mm(node, nw1_node) + mm(aggregate, nw1_agg) + nb1_ref[...]
    act, slope = silu_parts(pre)
    nw2 = nw2_ref[...]
    ng = ng_ref[...]
    normed, inv = norm_forward(mm(act, nw2), 1)
    fresh = (node.astype(F32) + normed * ng).astype(BF16)
    fresh_ref[...] = fresh

    coarse = coarse_cot_ref.shape[0]
    half = (0.5 * coarse_cot_ref[...].astype(F32)).astype(BF16)
    cell_row = iota((cells, coarse), 0)
    pooled = onehot((first_ref[...] == cell_row) | (second_ref[...] == cell_row))
    returned = same[:, 16:32, :].reshape(16 * peers, feature)
    hot_match = onehot_rows(column_of(match_ref[...]), cells)
    d_fresh = mm(pooled, half) + mm_tn(hot_match, returned)
    match_rows = mm(hot_match, fresh)

    d_out = norm_backward(d_fresh, normed, inv, ng, 1)
    grads_ref[899:900, :] = jnp.sum(d_fresh * normed, axis=0, keepdims=True)
    d_out_half = d_out.astype(BF16)
    grads_ref[768:896, :] = mm_tn(act, d_out_half)
    d_pre = mm_nt(d_out_half, nw2) * slope
    grads_ref[898:899, :] = jnp.sum(d_pre, axis=0, keepdims=True)
    d_pre_half = d_pre.astype(BF16)
    grads_ref[512:640, :] = mm_tn(node, d_pre_half)
    grads_ref[640:768, :] = mm_tn(aggregate, d_pre_half)
    d_node_ref[...] = d_fresh + mm_nt(d_pre_half, nw1_node)
    d_aggregate = mm_nt(nw1_agg, d_pre_half).astype(BF16)

    cot = jnp.where(live_row, cot_ref[...].astype(F32), 0.0)
    u = jnp.where(live_column, cot.T + mm(d_aggregate, oht_ref[wide:, :]), 0.0)
    d_out_half = norm_backward(u, edge_normed, edge_inv, eg, 0).astype(BF16)
    d_gain = fold_lanes(u * edge_normed)
    d_pre = mm(ew2, d_out_half) * edge_slope
    d_pre_half = d_pre.astype(BF16)
    d_edges_ref[...] = (cot + mm_tn(d_pre_half, ew1_edge_t)).astype(BF16)
    d_edges_copy = pltpu.make_async_copy(d_edges_ref, d_edges_out, out_sem.at[1])
    d_edges_copy.start()
    scattered = mm_nt(d_pre_half, oht_ref[...]).astype(BF16)
    d_table = mm(ew1_src, scattered[:, 0:wide]).T
    d_target = mm(ew1_dst, scattered[:, wide:]).T
    d_node_ref[...] += d_table[0:cells, :] + d_target

    grads_ref[0:128, :] = mm(d_pre_half, edges_ref[...]).T
    grads_ref[384:512, :] = mm_nt(edge_act, d_out_half)
    grads_ref[896:897, :] = jnp.sum(fold_lanes(d_pre).T, axis=0, keepdims=True)
    grads_ref[897:898, :] = jnp.sum(d_gain.T, axis=0, keepdims=True)
    grads_ref[900:, :] = jnp.zeros_like(grads_ref[900:, :])
    grads_ref[128:384, :] = mm_nt(d_pre_half, ends_ref[...]).T
    kinds = [
        d_table[cells + 8 * peers * k : cells + 8 * peers * (k + 1), :].reshape(peers, 8, feature)
        for k in range(3)
    ]
    slab = slab_in_plane()
    slabs = send_ref.shape[0] // peers
    share = GRAD_ROWS // (slabs * peers)
    blank = jnp.zeros((peers, 8, feature), F32)
    first_plane, last_plane = slab == 0, slab == slabs - 1
    heads = [
        [kinds[0], match_rows.reshape(peers, 16, feature)],
        [kinds[2], jnp.where(last_plane, kinds[2], 0.0), blank],
    ]
    heads += [[blank, blank, blank]] * (slabs - 3)
    heads += [[kinds[1], jnp.where(first_plane, kinds[1], 0.0), blank]]
    for step, head in enumerate(heads):
        to = lax.rem(slab + step, slabs)
        grads = grads_ref[pl.ds(pl.multiple_of(to * (peers * share), 8), peers * share), :]
        block = jnp.concatenate(head + [grads.reshape(peers, share, feature)], axis=1)
        send_ref[pl.ds(peers * to, peers)] = block.astype(BF16)
    edges_copy.wait()
    d_edges_copy.wait()


def unpack(recv_ref, w1_ref, w2_ref, nw1_ref, nw2_ref, b1_ref, g_ref, nb1_ref, ng_ref):
    start = 0
    for out_ref in (w1_ref, w2_ref, nw1_ref, nw2_ref):
        rows = out_ref.shape[0]
        out_ref[...] = recv_ref[start : start + rows, :].astype(F32)
        start += rows
    tail = recv_ref[start : start + 16, :].astype(F32)
    for k, out_ref in enumerate((b1_ref, g_ref, nb1_ref, ng_ref)):
        out_ref[...] = tail[k : k + 1, :]


def finish_kernel(
    recv_ref, planes_ref, d_node_ref, fresh_ref, intra_ref, bound_ref,
    pick_ref, first_ref, second_ref, grads_ref, d_out_ref, coarse_ref, *weight_refs,
):
    unpack(grads_ref, *weight_refs)
    peers = intra_ref.shape[0]
    slabs = recv_ref.shape[0] // peers
    planes = planes_ref.shape[0]
    cells, feature = d_node_ref.shape
    slab = slab_in_plane()
    plane = lax.axis_index("z")

    def block_of(y):
        return recv_ref[pl.ds(peers * y, peers)].astype(F32)

    def gradients(block):
        return block[:, 0:8, :].reshape(8 * peers, feature).astype(BF16)

    same = block_of(slab)
    hot = onehot_rows(column_of(intra_ref[...]), cells)
    total = mm_tn(hot, gradients(same))
    faces = bound_ref.shape[1]
    first_row = planes_ref.shape[1] - faces
    for k, step, edge in ((0, -1, slab == 0), (1, 1, slab == slabs - 1)):
        face_row = bound_ref[k : k + 1, :]
        direct = gradients(block_of(lax.rem(slab + step + slabs, slabs)))
        direct = jnp.where(edge, jnp.zeros_like(direct), direct)
        total = total + mm_tn(onehot_rows(face_column(face_row, pick_ref[k]), cells), direct)
        far = jnp.clip(plane + step, 0, planes - 1)
        passed = planes_ref[far, first_row:, :]
        passed = jnp.where(edge & (far != plane), passed, jnp.zeros_like(passed))
        total = total + mm_tn(onehot_rows(column_of(face_row), cells), passed)
    d_out_ref[...] = d_node_ref[...] + total
    partners = same[:, 8:24, :].reshape(16 * peers, feature).astype(BF16)
    coarse = coarse_ref.shape[0]
    cell_row = iota((cells, coarse), 0)
    near = onehot((first_ref[...] == cell_row) | (second_ref[...] == cell_row))
    far = onehot(second_ref[...] - cells == iota((16 * peers, coarse), 0))
    coarse_ref[...] = (0.5 * (mm_tn(near, fresh_ref[...]) + mm_tn(far, partners))).astype(BF16)


def call(kernel, out_shape, *args, scratch=(), smem=(), hbm=(), hbm_out=(), held=(), name=None, cost=None, mib=8):
    def space(i, far):
        return pltpu.HBM if i in far else pltpu.VMEM

    one = not isinstance(out_shape, tuple)
    outs = [pl.BlockSpec(memory_space=space(i, hbm_out)) for i in range(1 if one else len(out_shape))]
    args = [pltpu.with_memory_space_constraint(x, pltpu.HBM) if i in hbm or i in held else x for i, x in enumerate(args)]
    return pl.pallas_call(
        kernel,
        out_shape=out_shape,
        in_specs=[
            pl.BlockSpec(memory_space=pltpu.SMEM if i in smem else space(i, hbm)) for i in range(len(args))
        ],
        out_specs=outs[0] if one else tuple(outs),
        scratch_shapes=list(scratch),
        compiler_params=pltpu.CompilerParams(vmem_limit_bytes=mib * MIB),
        name=name,
        cost_estimate=cost,
    )(*args)


def shape_of(shape, dtype):
    return jax.ShapeDtypeStruct(shape, dtype)


def per_device(
    slabs, node, edges, edge_src, edge_dst, edge_count, intra_idx, bound_idx, cross_pick,
    match_send, pool_first, pool_second, edge_w1, edge_b1, edge_w2, edge_gain,
    node_w1, node_b1, node_w2, node_gain, edge_cot, coarse_cot,
):
    node, edges, edge_cot, coarse_cot = node[0, 0], edges[0, 0], edge_cot[0, 0], coarse_cot[0, 0]
    intra, bound, pick, match = intra_idx[0, 0], bound_idx[0, 0], cross_pick[0], match_send[0, 0]
    first, second = pool_first[0], pool_second[0]
    src, dst = edge_src[0], edge_dst[0]
    cells, feature = node.shape
    slots = edges.shape[0]
    coarse = coarse_cot.shape[0]
    peers = lax.axis_size("sub")
    planes = lax.axis_size("z")
    in_plane = slabs // planes
    dom = ("z", "y1", "y0")
    face = shape_of((8 * peers, feature), BF16)
    wide = -(-(cells + 24 * peers) // 256) * 256

    def swap(rows):
        pairs = [(i - 1, i) for i in range(2, slabs, 2)]
        return lax.ppermute(rows, dom, pairs + [(j, i) for i, j in pairs])

    def exchange(blocks, axes):
        return lax.all_to_all(blocks, axes, split_axis=0, concat_axis=0, tiled=True)

    passed = swap(call(face_kernel, face, node, bound, pick, held=range(3), name="faces"))
    far = (
        node, second, coarse_cot, src, dst, edge_w1, edge_b1[None], edges, edge_w2, edge_gain[None],
        node_w1, node_b1[None], node_w2, node_gain[None], first, match, edge_cot, intra, bound, pick,
    )
    sent, count, onward_pick, *near = call(
        send_kernel,
        (shape_of((2 * peers, FIRST, feature), BF16), shape_of((8, 128), jnp.int32), shape_of((16 * peers, 128), BF16))
        + tuple(shape_of(x.shape, x.dtype) for x in far),
        edge_count, intra, bound, pick, *far,
        smem=(0,), held=range(1, 4), hbm=range(4, 4 + len(far)),
        scratch=[pltpu.SemaphoreType.DMA((len(far),))],
        name="send",
        cost=pl.CostEstimate(flops=60_000_000, bytes_accessed=400_000, transcendentals=0),
    )
    passed = passed.reshape(peers, 8, feature)
    passed = jnp.concatenate([passed, passed], axis=0)
    sent = jnp.concatenate([sent[:, 0:8], passed, sent[:, 16:]], axis=1)
    received = exchange(sent, PAIR)

    new_edges, d_edges, d_node, fresh, sent = call(
        main_kernel,
        (
            shape_of((slots, feature), BF16),
            shape_of((slots, feature), BF16),
            shape_of((cells, feature), F32),
            shape_of((cells, feature), BF16),
            shape_of((in_plane * peers, HEAD + GRAD_ROWS // (in_plane * peers), feature), BF16),
        ),
        count, received, *near[:-3],
        hbm_out=(0, 1),
        scratch=[
            pltpu.VMEM((slots, feature), BF16),
            pltpu.VMEM((slots, feature), BF16),
            pltpu.VMEM((wide, feature), BF16),
            pltpu.VMEM((2 * feature, slots), BF16),
            pltpu.VMEM((wide + cells, slots), BF16),
            pltpu.VMEM((GRAD_ROWS, feature), F32),
            pltpu.SemaphoreType.DMA((2,)),
        ],
        name="layer",
        mib=28,
    )
    received = exchange(sent, PLANE)
    scale = 1.0 / math.sqrt(slabs * peers * slots)

    def total(blocks):
        return jnp.sum(blocks.astype(F32), axis=0)

    def copies(rows, count):
        return jnp.broadcast_to(rows, (count,) + rows.shape)

    ends = jnp.concatenate([received[0:peers, 8:16], received[-peers:, 8:16]], axis=0)
    onward = mm_tn(onward_pick, ends.reshape(16 * peers, feature))[0 : bound.shape[1]]
    rows = jnp.concatenate([total(received[:, HEAD:]), onward], axis=0).astype(BF16)
    by_plane = exchange(copies(rows, planes), "z")
    share = rows.shape[0] - onward.shape[0]
    rows = (total(by_plane[:, 0:share]) * scale).astype(BF16)
    grads = exchange(copies(rows, in_plane * peers), PLANE)
    row = shape_of((1, feature), F32)
    d_node, coarse_out, w1, w2, nw1, nw2, b1, g, nb1, ng = call(
        finish_kernel,
        (
            shape_of((cells, feature), F32),
            shape_of((coarse, feature), BF16),
            shape_of((3 * feature, feature), F32),
            shape_of((feature, feature), F32),
            shape_of((2 * feature, feature), F32),
            shape_of((feature, feature), F32),
            row, row, row, row,
        ),
        received, by_plane, d_node, fresh, *near[-3:], near[14], near[1], grads.reshape(GRAD_ROWS, feature),
        name="finish",
    )
    return (
        new_edges[None, None], coarse_out[None, None], d_node[None, None], d_edges[None, None],
        w1, b1[0], w2, g[0], nw1, nb1[0], nw2, ng[0],
    )


def solution(mesh):
    slabs, peers = mesh.shape["dom"], mesh.shape["sub"]
    devices = mesh.devices.reshape(slabs // 4, 2, 2, peers)
    dom = ("z", "y1", "y0")
    inner = Mesh(devices, dom + ("sub",))
    four, three = P(dom, "sub", None, None), P(dom, "sub", None)
    return jax.shard_map(
        functools.partial(per_device, slabs),
        mesh=inner,
        in_specs=(
            four, four, three, three, P(dom, "sub"), four, four, P("sub", None, None, None),
            four, three, three, P(), P(), P(), P(), P(), P(), P(), P(), four, four,
        ),
        out_specs=(four, four, four, four) + (P(),) * 8,
        check_vma=False,
    )
```

```python
import functools
import math

import jax
import jax.numpy as jnp
from jax import lax
from jax.experimental import pallas as pl
from jax.experimental.pallas import tpu as pltpu
from jax.sharding import Mesh
from jax.sharding import PartitionSpec as P

NORM_EPSILON = 1e-05
F32 = jnp.float32
BF16 = jnp.bfloat16
MIB = 1024 * 1024

PAIR = ("y0", "sub")
PLANE = ("y1", "y0", "sub")
FIRST = 32
HEAD = 24
GRAD_ROWS = 1024


def mm(a, b):
    return lax.dot_general(a, b, (((1,), (0,)), ((), ())), preferred_element_type=F32)


def mm_nt(a, b):
    return lax.dot_general(a, b, (((1,), (1,)), ((), ())), preferred_element_type=F32)


def mm_tn(a, b):
    return lax.dot_general(a, b, (((0,), (0,)), ((), ())), preferred_element_type=F32)


def iota(shape, dim):
    return lax.broadcasted_iota(jnp.int32, shape, dim)


def onehot(mask):
    return jnp.where(mask, 1.0, 0.0).astype(BF16)


def two_parts(x):
    high = x.astype(BF16)
    low = (x - high.astype(F32)).astype(BF16)
    return high, low


def column_of(ids):
    a, b = ids.shape
    spread = jnp.broadcast_to(ids[:, None, :], (a, b, b))
    keep = iota((a, b, b), 1) == iota((a, b, b), 2)
    return jnp.sum(jnp.where(keep, spread, 0), axis=2, keepdims=True).reshape(a * b, 1)


def face_column(face_row, pick):
    spot = column_of(pick)
    shape = (spot.shape[0], face_row.shape[1])
    keep = spot == iota(shape, 1)
    return jnp.sum(jnp.where(keep, jnp.broadcast_to(face_row, shape), 0), axis=1, keepdims=True)


def onehot_rows(column, width):
    return onehot(column == iota((column.shape[0], width), 1))


def slab_in_plane():
    return lax.axis_index("y1") * lax.axis_size("y0") + lax.axis_index("y0")


def picked_rows(node, bound_ref, pick_ref, side):
    face_row = jnp.where(side == 0, bound_ref[0:1, :], bound_ref[1:2, :])
    return mm(onehot_rows(face_column(face_row, pick_ref[side]), node.shape[0]), node)


def face_kernel(node_ref, bound_ref, pick_ref, out_ref):
    out_ref[...] = picked_rows(node_ref[...], bound_ref, pick_ref, lax.axis_index("y0")).astype(BF16)


def send_kernel(count_ref, *refs):
    arrays = (len(refs) - 4) // 2
    far, near, sem = refs[:arrays], refs[arrays + 3 : -1], refs[-1]
    out_ref, count_out_ref, onward_ref = refs[arrays : arrays + 3]
    copies = [pltpu.make_async_copy(far[k], near[k], sem.at[k]) for k in range(arrays)]
    for copy in copies:
        copy.start()
    node_ref, second_ref, coarse_cot_ref, intra_ref, bound_ref, pick_ref = near[0:6]
    count_out_ref[...] = jnp.full(count_out_ref.shape, count_ref[0, 0], jnp.int32)
    for copy in copies[0:6]:
        copy.wait()
    slab = slab_in_plane()
    last = lax.axis_size("y1") * lax.axis_size("y0") - 1
    half_rows = onward_ref.shape[0] // 2
    for k, reader in ((0, last), (1, 0)):
        column = jnp.where(slab == reader, column_of(pick_ref[1 - k]), -1)
        onward_ref[half_rows * k : half_rows * (k + 1), :] = onehot_rows(column, 128)
    odd = lax.axis_index("y0")
    node = node_ref[...]
    cells, feature = node.shape
    peers, halo = intra_ref.shape
    coarse = coarse_cot_ref.shape[0]
    intra = mm(onehot_rows(column_of(intra_ref[...]), cells), node)
    half = 0.5 * coarse_cot_ref[...].astype(F32)
    pool_rows = 16 * peers
    pool = mm(onehot(second_ref[...] - cells == iota((pool_rows, coarse), 0)), half.astype(BF16))
    same = [
        intra.reshape(peers, halo, feature),
        jnp.zeros((peers, halo, feature), F32),
        pool.reshape(peers, 16, feature),
    ]
    other = [
        picked_rows(node, bound_ref, pick_ref, 1 - odd).reshape(peers, halo, feature),
        jnp.zeros((peers, FIRST - halo, feature), F32),
    ]
    out_ref[pl.ds(peers * odd, peers)] = jnp.concatenate(same, axis=1).astype(BF16)
    out_ref[pl.ds(peers * (1 - odd), peers)] = jnp.concatenate(other, axis=1).astype(BF16)
    for copy in copies[6:]:
        copy.wait()


def silu_parts(pre):
    sig = 0.5 * jnp.tanh(0.5 * pre) + 0.5
    act = (pre * sig).astype(BF16)
    slope = sig * (1.0 + pre * (1.0 - sig))
    return act, slope


def norm_forward(out, axis):
    centred = out - jnp.mean(out, axis=axis, keepdims=True)
    inv = lax.rsqrt(jnp.mean(centred * centred, axis=axis, keepdims=True) + NORM_EPSILON)
    return centred * inv, inv


def norm_backward(u, normed, inv, gain, axis):
    scaled = u * gain
    inner = (
        scaled
        - jnp.mean(scaled, axis=axis, keepdims=True)
        - normed * jnp.mean(scaled * normed, axis=axis, keepdims=True)
    )
    return inner * inv


def fold_lanes(x):
    total = x[:, 0:128]
    for k in range(1, x.shape[1] // 128):
        total = total + x[:, 128 * k : 128 * k + 128]
    return total


def column_block(row, width):
    block = jnp.broadcast_to(row, (128, 128)).T
    return jnp.concatenate([block] * (width // 128), axis=1)


def hot_columns(ids, rows):
    width = ids.shape[1]

    def spread(x):
        return jnp.broadcast_to(x.astype(F32), (16, width)).astype(BF16)

    tens, units = spread(ids & -16), spread(ids & 15)
    zero = jnp.zeros((16, width), BF16)
    base = jnp.where(units == iota((16, width), 0).astype(F32).astype(BF16), jnp.ones((16, width), BF16), zero)
    return jnp.concatenate(
        [jnp.where(tens == jnp.full((16, width), 16 * r, BF16), base, zero) for r in range(rows // 16)], axis=0
    )


def main_kernel(
    count_ref, recv_ref, node_ref, second_ref, coarse_cot_ref, src_ref, dst_ref, ew1_ref, eb1_ref, edges_ref,
    ew2_ref, eg_ref, nw1_ref, nb1_ref, nw2_ref, ng_ref, first_ref, match_ref, cot_ref,
    new_edges_out, d_edges_out, d_node_ref, fresh_ref, send_ref,
    new_edges_ref, d_edges_ref, table_ref, ends_ref, oht_ref, grads_ref, out_sem,
):
    cells, feature = node_ref.shape
    wide = table_ref.shape[0]
    oht_ref[0:wide, :] = hot_columns(src_ref[...], wide)
    oht_ref[wide:, :] = hot_columns(dst_ref[...], cells)
    slots = edges_ref.shape[0]
    peers = recv_ref.shape[0] // 2
    count = count_ref[0:1, 0:1]
    node = node_ref[...]
    odd = lax.axis_index("y0")
    same = recv_ref[pl.ds(peers * odd, peers)]
    near = same.astype(F32)
    other = recv_ref[pl.ds(peers * (1 - odd), peers)].astype(F32)[:, 0:8, :]
    passed = near[:, 8:16, :]
    kinds = [near[:, 0:8, :], jnp.where(odd == 0, passed, other), jnp.where(odd == 0, other, passed)]
    halo_rows = 3 * 8 * peers
    table_ref[0:cells, :] = node
    halo = jnp.concatenate(
        [rows.reshape(8 * peers, feature) for rows in kinds]
        + [jnp.zeros((wide - cells - halo_rows, feature), F32)],
        axis=0,
    )
    table_ref[cells:wide, :] = halo.astype(BF16)
    ew1_edge_t = ew1_ref[0:feature, :].T
    ew1_src = ew1_ref[feature : 2 * feature, :]
    ew1_dst = ew1_ref[2 * feature : 3 * feature, :]
    ew2 = ew2_ref[...]
    eg = column_block(eg_ref[...], slots)
    live_column = iota((feature, slots), 1) < count
    live_row = iota((slots, feature), 0) < count

    ends_ref[0:feature, :] = mm(table_ref[...].T, oht_ref[0:wide, :]).astype(BF16)
    ends_ref[feature:, :] = mm(node.T, oht_ref[wide:, :]).astype(BF16)
    pre = mm(ew1_ref[feature:, :].T, ends_ref[...]) + mm_nt(ew1_edge_t, edges_ref[...])
    pre = pre + column_block(eb1_ref[...], slots)
    edge_act, edge_slope = silu_parts(pre)
    edge_normed, edge_inv = norm_forward(mm(ew2.T, edge_act), 0)
    message = jnp.where(live_column, edge_normed * eg, 0.0)
    new_edges = jnp.where(live_row, edges_ref[...].astype(F32) + message.T, 0.0)
    new_edges_ref[...] = new_edges.astype(BF16)
    edges_copy = pltpu.make_async_copy(new_edges_ref, new_edges_out, out_sem.at[0])
    edges_copy.start()
    both = mm_nt(jnp.concatenate(two_parts(message), axis=0), oht_ref[wide:, :])
    aggregate = (both[0:feature] + both[feature:]).T.astype(BF16)

    nw1_node = nw1_ref[0:feature, :]
    nw1_agg = nw1_ref[feature:, :]
    pre = mm(node, nw1_node) + mm(aggregate, nw1_agg) + nb1_ref[...]
    act, slope = silu_parts(pre)
    nw2 = nw2_ref[...]
    ng = ng_ref[...]
    normed, inv = norm_forward(mm(act, nw2), 1)
    fresh = (node.astype(F32) + normed * ng).astype(BF16)
    fresh_ref[...] = fresh

    coarse = coarse_cot_ref.shape[0]
    half = (0.5 * coarse_cot_ref[...].astype(F32)).astype(BF16)
    cell_row = iota((cells, coarse), 0)
    pooled = onehot((first_ref[...] == cell_row) | (second_ref[...] == cell_row))
    returned = same[:, 16:32, :].reshape(16 * peers, feature)
    hot_match = onehot_rows(column_of(match_ref[...]), cells)
    d_fresh = mm(pooled, half) + mm_tn(hot_match, returned)
    match_rows = mm(hot_match, fresh)

    d_out = norm_backward(d_fresh, normed, inv, ng, 1)
    grads_ref[899:900, :] = jnp.sum(d_fresh * normed, axis=0, keepdims=True)
    d_out_half = d_out.astype(BF16)
    grads_ref[768:896, :] = mm_tn(act, d_out_half)
    d_pre = mm_nt(d_out_half, nw2) * slope
    grads_ref[898:899, :] = jnp.sum(d_pre, axis=0, keepdims=True)
    d_pre_half = d_pre.astype(BF16)
    grads_ref[512:640, :] = mm_tn(node, d_pre_half)
    grads_ref[640:768, :] = mm_tn(aggregate, d_pre_half)
    d_node_ref[...] = d_fresh + mm_nt(d_pre_half, nw1_node)
    d_aggregate = mm_nt(nw1_agg, d_pre_half).astype(BF16)

    cot = jnp.where(live_row, cot_ref[...].astype(F32), 0.0)
    u = jnp.where(live_column, cot.T + mm(d_aggregate, oht_ref[wide:, :]), 0.0)
    d_out_half = norm_backward(u, edge_normed, edge_inv, eg, 0).astype(BF16)
    d_gain = fold_lanes(u * edge_normed)
    d_pre = mm(ew2, d_out_half) * edge_slope
    d_pre_half = d_pre.astype(BF16)
    d_edges_ref[...] = (cot + mm_tn(d_pre_half, ew1_edge_t)).astype(BF16)
    d_edges_copy = pltpu.make_async_copy(d_edges_ref, d_edges_out, out_sem.at[1])
    d_edges_copy.start()
    scattered = mm_nt(d_pre_half, oht_ref[...]).astype(BF16)
    d_table = mm(ew1_src, scattered[:, 0:wide]).T
    d_target = mm(ew1_dst, scattered[:, wide:]).T
    d_node_ref[...] += d_table[0:cells, :] + d_target

    grads_ref[0:128, :] = mm(d_pre_half, edges_ref[...]).T
    grads_ref[384:512, :] = mm_nt(edge_act, d_out_half)
    grads_ref[896:897, :] = jnp.sum(fold_lanes(d_pre).T, axis=0, keepdims=True)
    grads_ref[897:898, :] = jnp.sum(d_gain.T, axis=0, keepdims=True)
    grads_ref[900:, :] = jnp.zeros_like(grads_ref[900:, :])
    grads_ref[128:384, :] = mm_nt(d_pre_half, ends_ref[...]).T
    kinds = [
        d_table[cells + 8 * peers * k : cells + 8 * peers * (k + 1), :].reshape(peers, 8, feature)
        for k in range(3)
    ]
    slab = slab_in_plane()
    slabs = send_ref.shape[0] // peers
    share = GRAD_ROWS // (slabs * peers)
    blank = jnp.zeros((peers, 8, feature), F32)
    first_plane, last_plane = slab == 0, slab == slabs - 1
    heads = [
        [kinds[0], match_rows.reshape(peers, 16, feature)],
        [kinds[2], jnp.where(last_plane, kinds[2], 0.0), blank],
    ]
    heads += [[blank, blank, blank]] * (slabs - 3)
    heads += [[kinds[1], jnp.where(first_plane, kinds[1], 0.0), blank]]
    for step, head in enumerate(heads):
        to = lax.rem(slab + step, slabs)
        grads = grads_ref[pl.ds(pl.multiple_of(to * (peers * share), 8), peers * share), :]
        block = jnp.concatenate(head + [grads.reshape(peers, share, feature)], axis=1)
        send_ref[pl.ds(peers * to, peers)] = block.astype(BF16)
    edges_copy.wait()
    d_edges_copy.wait()


def unpack(recv_ref, w1_ref, w2_ref, nw1_ref, nw2_ref, b1_ref, g_ref, nb1_ref, ng_ref):
    start = 0
    for out_ref in (w1_ref, w2_ref, nw1_ref, nw2_ref):
        rows = out_ref.shape[0]
        out_ref[...] = recv_ref[start : start + rows, :].astype(F32)
        start += rows
    tail = recv_ref[start : start + 16, :].astype(F32)
    for k, out_ref in enumerate((b1_ref, g_ref, nb1_ref, ng_ref)):
        out_ref[...] = tail[k : k + 1, :]


def finish_kernel(
    recv_ref, planes_ref, d_node_ref, fresh_ref, intra_ref, bound_ref,
    pick_ref, first_ref, second_ref, grads_ref, d_out_ref, coarse_ref, *weight_refs,
):
    unpack(grads_ref, *weight_refs)
    peers = intra_ref.shape[0]
    slabs = recv_ref.shape[0] // peers
    planes = planes_ref.shape[0]
    cells, feature = d_node_ref.shape
    slab = slab_in_plane()
    plane = lax.axis_index("z")

    def block_of(y):
        return recv_ref[pl.ds(peers * y, peers)].astype(F32)

    def gradients(block):
        return block[:, 0:8, :].reshape(8 * peers, feature).astype(BF16)

    same = block_of(slab)
    hot = onehot_rows(column_of(intra_ref[...]), cells)
    total = mm_tn(hot, gradients(same))
    faces = bound_ref.shape[1]
    first_row = planes_ref.shape[1] - faces
    for k, step, edge in ((0, -1, slab == 0), (1, 1, slab == slabs - 1)):
        face_row = bound_ref[k : k + 1, :]
        direct = gradients(block_of(lax.rem(slab + step + slabs, slabs)))
        direct = jnp.where(edge, jnp.zeros_like(direct), direct)
        total = total + mm_tn(onehot_rows(face_column(face_row, pick_ref[k]), cells), direct)
        far = jnp.clip(plane + step, 0, planes - 1)
        passed = planes_ref[far, first_row:, :]
        passed = jnp.where(edge & (far != plane), passed, jnp.zeros_like(passed))
        total = total + mm_tn(onehot_rows(column_of(face_row), cells), passed)
    d_out_ref[...] = d_node_ref[...] + total
    partners = same[:, 8:24, :].reshape(16 * peers, feature).astype(BF16)
    coarse = coarse_ref.shape[0]
    cell_row = iota((cells, coarse), 0)
    near = onehot((first_ref[...] == cell_row) | (second_ref[...] == cell_row))
    far = onehot(second_ref[...] - cells == iota((16 * peers, coarse), 0))
    coarse_ref[...] = (0.5 * (mm_tn(near, fresh_ref[...]) + mm_tn(far, partners))).astype(BF16)


def call(kernel, out_shape, *args, scratch=(), smem=(), hbm=(), hbm_out=(), held=(), name=None, cost=None, mib=8):
    def space(i, far):
        return pltpu.HBM if i in far else pltpu.VMEM

    one = not isinstance(out_shape, tuple)
    outs = [pl.BlockSpec(memory_space=space(i, hbm_out)) for i in range(1 if one else len(out_shape))]
    args = [pltpu.with_memory_space_constraint(x, pltpu.HBM) if i in hbm or i in held else x for i, x in enumerate(args)]
    return pl.pallas_call(
        kernel,
        out_shape=out_shape,
        in_specs=[
            pl.BlockSpec(memory_space=pltpu.SMEM if i in smem else space(i, hbm)) for i in range(len(args))
        ],
        out_specs=outs[0] if one else tuple(outs),
        scratch_shapes=list(scratch),
        compiler_params=pltpu.CompilerParams(vmem_limit_bytes=mib * MIB),
        name=name,
        cost_estimate=cost,
    )(*args)


def shape_of(shape, dtype):
    return jax.ShapeDtypeStruct(shape, dtype)


def per_device(
    slabs, node, edges, edge_src, edge_dst, edge_count, intra_idx, bound_idx, cross_pick,
    match_send, pool_first, pool_second, edge_w1, edge_b1, edge_w2, edge_gain,
    node_w1, node_b1, node_w2, node_gain, edge_cot, coarse_cot,
):
    node, edges, edge_cot, coarse_cot = node[0, 0], edges[0, 0], edge_cot[0, 0], coarse_cot[0, 0]
    intra, bound, pick, match = intra_idx[0, 0], bound_idx[0, 0], cross_pick[0], match_send[0, 0]
    first, second = pool_first[0], pool_second[0]
    src, dst = edge_src[0], edge_dst[0]
    cells, feature = node.shape
    slots = edges.shape[0]
    coarse = coarse_cot.shape[0]
    peers = lax.axis_size("sub")
    planes = lax.axis_size("z")
    in_plane = slabs // planes
    dom = ("z", "y1", "y0")
    face = shape_of((8 * peers, feature), BF16)
    wide = -(-(cells + 24 * peers) // 256) * 256

    def swap(rows):
        pairs = [(i - 1, i) for i in range(2, slabs, 2)]
        return lax.ppermute(rows, dom, pairs + [(j, i) for i, j in pairs])

    def exchange(blocks, axes):
        return lax.all_to_all(blocks, axes, split_axis=0, concat_axis=0, tiled=True)

    passed = swap(call(face_kernel, face, node, bound, pick, held=range(3), name="faces"))
    far = (
        node, second, coarse_cot, intra, bound, pick, src, dst, edge_w1, edge_b1[None], edges, edge_w2,
        edge_gain[None], node_w1, node_b1[None], node_w2, node_gain[None], first, match, edge_cot,
    )
    sent, count, onward_pick, *near = call(
        send_kernel,
        (shape_of((2 * peers, FIRST, feature), BF16), shape_of((8, 128), jnp.int32), shape_of((16 * peers, 128), BF16))
        + tuple(shape_of(x.shape, x.dtype) for x in far),
        edge_count, *far,
        smem=(0,), hbm=range(1, 1 + len(far)),
        scratch=[pltpu.SemaphoreType.DMA((len(far),))],
        name="send",
        cost=pl.CostEstimate(flops=60_000_000, bytes_accessed=400_000, transcendentals=0),
    )
    passed = passed.reshape(peers, 8, feature)
    passed = jnp.concatenate([passed, passed], axis=0)
    sent = jnp.concatenate([sent[:, 0:8], passed, sent[:, 16:]], axis=1)
    received = exchange(sent, PAIR)

    new_edges, d_edges, d_node, fresh, sent = call(
        main_kernel,
        (
            shape_of((slots, feature), BF16),
            shape_of((slots, feature), BF16),
            shape_of((cells, feature), F32),
            shape_of((cells, feature), BF16),
            shape_of((in_plane * peers, HEAD + GRAD_ROWS // (in_plane * peers), feature), BF16),
        ),
        count, received, *near[0:3], *near[6:],
        hbm_out=(0, 1),
        scratch=[
            pltpu.VMEM((slots, feature), BF16),
            pltpu.VMEM((slots, feature), BF16),
            pltpu.VMEM((wide, feature), BF16),
            pltpu.VMEM((2 * feature, slots), BF16),
            pltpu.VMEM((wide + cells, slots), BF16),
            pltpu.VMEM((GRAD_ROWS, feature), F32),
            pltpu.SemaphoreType.DMA((2,)),
        ],
        name="layer",
        mib=28,
    )
    received = exchange(sent, PLANE)
    scale = 1.0 / math.sqrt(slabs * peers * slots)

    def total(blocks):
        return jnp.sum(blocks.astype(F32), axis=0)

    def copies(rows, count):
        return jnp.broadcast_to(rows, (count,) + rows.shape)

    ends = jnp.concatenate([received[0:peers, 8:16], received[-peers:, 8:16]], axis=0)
    onward = mm_tn(onward_pick, ends.reshape(16 * peers, feature))[0 : bound.shape[1]]
    rows = jnp.concatenate([total(received[:, HEAD:]), onward], axis=0).astype(BF16)
    by_plane = exchange(copies(rows, planes), "z")
    share = rows.shape[0] - onward.shape[0]
    rows = (total(by_plane[:, 0:share]) * scale).astype(BF16)
    grads = exchange(copies(rows, in_plane * peers), PLANE)
    row = shape_of((1, feature), F32)
    d_node, coarse_out, w1, w2, nw1, nw2, b1, g, nb1, ng = call(
        finish_kernel,
        (
            shape_of((cells, feature), F32),
            shape_of((coarse, feature), BF16),
            shape_of((3 * feature, feature), F32),
            shape_of((feature, feature), F32),
            shape_of((2 * feature, feature), F32),
            shape_of((feature, feature), F32),
            row, row, row, row,
        ),
        received, by_plane, d_node, fresh, *near[3:6], near[17], near[1], grads.reshape(GRAD_ROWS, feature),
        name="finish",
    )
    return (
        new_edges[None, None], coarse_out[None, None], d_node[None, None], d_edges[None, None],
        w1, b1[0], w2, g[0], nw1, nb1[0], nw2, ng[0],
    )


def solution(mesh):
    slabs, peers = mesh.shape["dom"], mesh.shape["sub"]
    devices = mesh.devices.reshape(slabs // 4, 2, 2, peers)
    dom = ("z", "y1", "y0")
    inner = Mesh(devices, dom + ("sub",))
    four, three = P(dom, "sub", None, None), P(dom, "sub", None)
    return jax.shard_map(
        functools.partial(per_device, slabs),
        mesh=inner,
        in_specs=(
            four, four, three, three, P(dom, "sub"), four, four, P("sub", None, None, None),
            four, three, three, P(), P(), P(), P(), P(), P(), P(), P(), four, four,
        ),
        out_specs=(four, four, four, four) + (P(),) * 8,
        check_vma=False,
    )
```

```python
import functools
import math

import jax
import jax.numpy as jnp
from jax import lax
from jax.experimental import pallas as pl
from jax.experimental.pallas import tpu as pltpu
from jax.sharding import Mesh
from jax.sharding import PartitionSpec as P

NORM_EPSILON = 1e-05
F32 = jnp.float32
BF16 = jnp.bfloat16
MIB = 1024 * 1024

PAIR = ("y0", "sub")
PLANE = ("y1", "y0", "sub")
FIRST = 32
HEAD = 24
GRAD_ROWS = 1024


def mm(a, b):
    return lax.dot_general(a, b, (((1,), (0,)), ((), ())), preferred_element_type=F32)


def mm_nt(a, b):
    return lax.dot_general(a, b, (((1,), (1,)), ((), ())), preferred_element_type=F32)


def mm_tn(a, b):
    return lax.dot_general(a, b, (((0,), (0,)), ((), ())), preferred_element_type=F32)


def iota(shape, dim):
    return lax.broadcasted_iota(jnp.int32, shape, dim)


def onehot(mask):
    return jnp.where(mask, 1.0, 0.0).astype(BF16)


def two_parts(x):
    high = x.astype(BF16)
    low = (x - high.astype(F32)).astype(BF16)
    return high, low


def column_of(ids):
    a, b = ids.shape
    spread = jnp.broadcast_to(ids[:, None, :], (a, b, b))
    keep = iota((a, b, b), 1) == iota((a, b, b), 2)
    return jnp.sum(jnp.where(keep, spread, 0), axis=2, keepdims=True).reshape(a * b, 1)


def face_column(face_row, pick):
    spot = column_of(pick)
    shape = (spot.shape[0], face_row.shape[1])
    keep = spot == iota(shape, 1)
    return jnp.sum(jnp.where(keep, jnp.broadcast_to(face_row, shape), 0), axis=1, keepdims=True)


def onehot_rows(column, width):
    return onehot(column == iota((column.shape[0], width), 1))


def slab_in_plane():
    return lax.axis_index("y1") * lax.axis_size("y0") + lax.axis_index("y0")


def picked_rows(node, bound_ref, pick_ref, side):
    face_row = jnp.where(side == 0, bound_ref[0:1, :], bound_ref[1:2, :])
    return mm(onehot_rows(face_column(face_row, pick_ref[side]), node.shape[0]), node)


def face_kernel(node_ref, bound_ref, pick_ref, out_ref):
    out_ref[...] = picked_rows(node_ref[...], bound_ref, pick_ref, lax.axis_index("y0")).astype(BF16)


def send_kernel(count_ref, *refs):
    arrays = (len(refs) - 4) // 2
    far, near, sem = refs[:arrays], refs[arrays + 3 : -1], refs[-1]
    out_ref, count_out_ref, onward_ref = refs[arrays : arrays + 3]
    copies = [pltpu.make_async_copy(far[k], near[k], sem.at[k]) for k in range(arrays)]
    for copy in copies:
        copy.start()
    node_ref, second_ref, coarse_cot_ref, intra_ref, bound_ref, pick_ref = near[0:6]
    count_out_ref[...] = jnp.full(count_out_ref.shape, count_ref[0, 0], jnp.int32)
    for copy in copies[0:6]:
        copy.wait()
    slab = slab_in_plane()
    last = lax.axis_size("y1") * lax.axis_size("y0") - 1
    half_rows = onward_ref.shape[0] // 2
    for k, reader in ((0, last), (1, 0)):
        column = jnp.where(slab == reader, column_of(pick_ref[1 - k]), -1)
        onward_ref[half_rows * k : half_rows * (k + 1), :] = onehot_rows(column, 128)
    odd = lax.axis_index("y0")
    node = node_ref[...]
    cells, feature = node.shape
    peers, halo = intra_ref.shape
    coarse = coarse_cot_ref.shape[0]
    intra = mm(onehot_rows(column_of(intra_ref[...]), cells), node)
    half = 0.5 * coarse_cot_ref[...].astype(F32)
    pool_rows = 16 * peers
    pool = mm(onehot(second_ref[...] - cells == iota((pool_rows, coarse), 0)), half.astype(BF16))
    same = [
        intra.reshape(peers, halo, feature),
        jnp.zeros((peers, halo, feature), F32),
        pool.reshape(peers, 16, feature),
    ]
    other = [
        picked_rows(node, bound_ref, pick_ref, 1 - odd).reshape(peers, halo, feature),
        jnp.zeros((peers, FIRST - halo, feature), F32),
    ]
    out_ref[pl.ds(peers * odd, peers)] = jnp.concatenate(same, axis=1).astype(BF16)
    out_ref[pl.ds(peers * (1 - odd), peers)] = jnp.concatenate(other, axis=1).astype(BF16)
    for copy in copies[6:]:
        copy.wait()


def silu_parts(pre):
    sig = 0.5 * jnp.tanh(0.5 * pre) + 0.5
    act = (pre * sig).astype(BF16)
    slope = sig * (1.0 + pre * (1.0 - sig))
    return act, slope


def norm_forward(out, axis):
    centred = out - jnp.mean(out, axis=axis, keepdims=True)
    inv = lax.rsqrt(jnp.mean(centred * centred, axis=axis, keepdims=True) + NORM_EPSILON)
    return centred * inv, inv


def norm_backward(u, normed, inv, gain, axis):
    scaled = u * gain
    inner = (
        scaled
        - jnp.mean(scaled, axis=axis, keepdims=True)
        - normed * jnp.mean(scaled * normed, axis=axis, keepdims=True)
    )
    return inner * inv


def fold_lanes(x):
    total = x[:, 0:128]
    for k in range(1, x.shape[1] // 128):
        total = total + x[:, 128 * k : 128 * k + 128]
    return total


def column_block(row, width):
    block = jnp.broadcast_to(row, (128, 128)).T
    return jnp.concatenate([block] * (width // 128), axis=1)


def hot_columns(ids, rows):
    width = ids.shape[1]

    def spread(x):
        return jnp.broadcast_to(x.astype(F32), (16, width)).astype(BF16)

    tens, units = spread(ids & -16), spread(ids & 15)
    zero = jnp.zeros((16, width), BF16)
    base = jnp.where(units == iota((16, width), 0).astype(F32).astype(BF16), jnp.ones((16, width), BF16), zero)
    return jnp.concatenate(
        [jnp.where(tens == jnp.full((16, width), 16 * r, BF16), base, zero) for r in range(rows // 16)], axis=0
    )


def main_kernel(
    count_ref, recv_ref, node_ref, second_ref, coarse_cot_ref, src_ref, dst_ref, ew1_ref, eb1_ref, edges_ref,
    ew2_ref, eg_ref, nw1_ref, nb1_ref, nw2_ref, ng_ref, first_ref, match_ref, cot_ref,
    new_edges_out, d_edges_out, d_node_ref, fresh_ref, send_ref,
    new_edges_ref, d_edges_ref, table_ref, ends_ref, oht_ref, grads_ref, out_sem,
):
    cells, feature = node_ref.shape
    wide = table_ref.shape[0]
    oht_ref[0:wide, :] = hot_columns(src_ref[...], wide)
    oht_ref[wide:, :] = hot_columns(dst_ref[...], cells)
    slots = edges_ref.shape[0]
    peers = recv_ref.shape[0] // 2
    count = count_ref[0:1, 0:1]
    node = node_ref[...]
    odd = lax.axis_index("y0")
    same = recv_ref[pl.ds(peers * odd, peers)]
    near = same.astype(F32)
    other = recv_ref[pl.ds(peers * (1 - odd), peers)].astype(F32)[:, 0:8, :]
    passed = near[:, 8:16, :]
    kinds = [near[:, 0:8, :], jnp.where(odd == 0, passed, other), jnp.where(odd == 0, other, passed)]
    halo_rows = 3 * 8 * peers
    table_ref[0:cells, :] = node
    halo = jnp.concatenate(
        [rows.reshape(8 * peers, feature) for rows in kinds]
        + [jnp.zeros((wide - cells - halo_rows, feature), F32)],
        axis=0,
    )
    table_ref[cells:wide, :] = halo.astype(BF16)
    ew1_edge_t = ew1_ref[0:feature, :].T
    ew1_src = ew1_ref[feature : 2 * feature, :]
    ew1_dst = ew1_ref[2 * feature : 3 * feature, :]
    ew2 = ew2_ref[...]
    eg = column_block(eg_ref[...], slots)
    live_column = iota((feature, slots), 1) < count
    live_row = iota((slots, feature), 0) < count

    ends_ref[0:feature, :] = mm(table_ref[...].T, oht_ref[0:wide, :]).astype(BF16)
    ends_ref[feature:, :] = mm(node.T, oht_ref[wide:, :]).astype(BF16)
    pre = mm(ew1_ref[feature:, :].T, ends_ref[...]) + mm_nt(ew1_edge_t, edges_ref[...])
    pre = pre + column_block(eb1_ref[...], slots)
    edge_act, edge_slope = silu_parts(pre)
    edge_normed, edge_inv = norm_forward(mm(ew2.T, edge_act), 0)
    message = jnp.where(live_column, edge_normed * eg, 0.0)
    new_edges = jnp.where(live_row, edges_ref[...].astype(F32) + message.T, 0.0)
    new_edges_ref[...] = new_edges.astype(BF16)
    edges_copy = pltpu.make_async_copy(new_edges_ref, new_edges_out, out_sem.at[0])
    edges_copy.start()
    aggregate = mm_nt(message.astype(BF16), oht_ref[wide:, :]).T.astype(BF16)

    nw1_node = nw1_ref[0:feature, :]
    nw1_agg = nw1_ref[feature:, :]
    pre = mm(node, nw1_node) + mm(aggregate, nw1_agg) + nb1_ref[...]
    act, slope = silu_parts(pre)
    nw2 = nw2_ref[...]
    ng = ng_ref[...]
    normed, inv = norm_forward(mm(act, nw2), 1)
    fresh = (node.astype(F32) + normed * ng).astype(BF16)
    fresh_ref[...] = fresh

    coarse = coarse_cot_ref.shape[0]
    half = (0.5 * coarse_cot_ref[...].astype(F32)).astype(BF16)
    cell_row = iota((cells, coarse), 0)
    pooled = onehot((first_ref[...] == cell_row) | (second_ref[...] == cell_row))
    returned = same[:, 16:32, :].reshape(16 * peers, feature)
    hot_match = onehot_rows(column_of(match_ref[...]), cells)
    d_fresh = mm(pooled, half) + mm_tn(hot_match, returned)
    match_rows = mm(hot_match, fresh)

    d_out = norm_backward(d_fresh, normed, inv, ng, 1)
    grads_ref[899:900, :] = jnp.sum(d_fresh * normed, axis=0, keepdims=True)
    d_out_half = d_out.astype(BF16)
    grads_ref[768:896, :] = mm_tn(act, d_out_half)
    d_pre = mm_nt(d_out_half, nw2) * slope
    grads_ref[898:899, :] = jnp.sum(d_pre, axis=0, keepdims=True)
    d_pre_half = d_pre.astype(BF16)
    grads_ref[512:640, :] = mm_tn(node, d_pre_half)
    grads_ref[640:768, :] = mm_tn(aggregate, d_pre_half)
    d_node_ref[...] = d_fresh + mm_nt(d_pre_half, nw1_node)
    d_aggregate = mm_nt(nw1_agg, d_pre_half).astype(BF16)

    cot = jnp.where(live_row, cot_ref[...].astype(F32), 0.0)
    u = jnp.where(live_column, cot.T + mm(d_aggregate, oht_ref[wide:, :]), 0.0)
    d_out_half = norm_backward(u, edge_normed, edge_inv, eg, 0).astype(BF16)
    d_gain = fold_lanes(u * edge_normed)
    d_pre = mm(ew2, d_out_half) * edge_slope
    d_pre_half = d_pre.astype(BF16)
    d_edges_ref[...] = (cot + mm_tn(d_pre_half, ew1_edge_t)).astype(BF16)
    d_edges_copy = pltpu.make_async_copy(d_edges_ref, d_edges_out, out_sem.at[1])
    d_edges_copy.start()
    scattered = mm_nt(d_pre_half, oht_ref[...]).astype(BF16)
    d_table = mm(ew1_src, scattered[:, 0:wide]).T
    d_target = mm(ew1_dst, scattered[:, wide:]).T
    d_node_ref[...] += d_table[0:cells, :] + d_target

    grads_ref[0:128, :] = mm(d_pre_half, edges_ref[...]).T
    grads_ref[384:512, :] = mm_nt(edge_act, d_out_half)
    grads_ref[896:897, :] = jnp.sum(fold_lanes(d_pre).T, axis=0, keepdims=True)
    grads_ref[897:898, :] = jnp.sum(d_gain.T, axis=0, keepdims=True)
    grads_ref[900:, :] = jnp.zeros_like(grads_ref[900:, :])
    grads_ref[128:384, :] = mm_nt(d_pre_half, ends_ref[...]).T
    kinds = [
        d_table[cells + 8 * peers * k : cells + 8 * peers * (k + 1), :].reshape(peers, 8, feature)
        for k in range(3)
    ]
    slab = slab_in_plane()
    slabs = send_ref.shape[0] // peers
    share = GRAD_ROWS // (slabs * peers)
    blank = jnp.zeros((peers, 8, feature), F32)
    first_plane, last_plane = slab == 0, slab == slabs - 1
    heads = [
        [kinds[0], match_rows.reshape(peers, 16, feature)],
        [kinds[2], jnp.where(last_plane, kinds[2], 0.0), blank],
    ]
    heads += [[blank, blank, blank]] * (slabs - 3)
    heads += [[kinds[1], jnp.where(first_plane, kinds[1], 0.0), blank]]
    for step, head in enumerate(heads):
        to = lax.rem(slab + step, slabs)
        grads = grads_ref[pl.ds(pl.multiple_of(to * (peers * share), 8), peers * share), :]
        block = jnp.concatenate(head + [grads.reshape(peers, share, feature)], axis=1)
        send_ref[pl.ds(peers * to, peers)] = block.astype(BF16)
    edges_copy.wait()
    d_edges_copy.wait()


def unpack(recv_ref, w1_ref, w2_ref, nw1_ref, nw2_ref, b1_ref, g_ref, nb1_ref, ng_ref):
    start = 0
    for out_ref in (w1_ref, w2_ref, nw1_ref, nw2_ref):
        rows = out_ref.shape[0]
        out_ref[...] = recv_ref[start : start + rows, :].astype(F32)
        start += rows
    tail = recv_ref[start : start + 16, :].astype(F32)
    for k, out_ref in enumerate((b1_ref, g_ref, nb1_ref, ng_ref)):
        out_ref[...] = tail[k : k + 1, :]


def finish_kernel(
    recv_ref, planes_ref, d_node_ref, fresh_ref, intra_ref, bound_ref,
    pick_ref, first_ref, second_ref, grads_ref, d_out_ref, coarse_ref, *weight_refs,
):
    unpack(grads_ref, *weight_refs)
    peers = intra_ref.shape[0]
    slabs = recv_ref.shape[0] // peers
    planes = planes_ref.shape[0]
    cells, feature = d_node_ref.shape
    slab = slab_in_plane()
    plane = lax.axis_index("z")

    def block_of(y):
        return recv_ref[pl.ds(peers * y, peers)].astype(F32)

    def gradients(block):
        return block[:, 0:8, :].reshape(8 * peers, feature).astype(BF16)

    same = block_of(slab)
    hot = onehot_rows(column_of(intra_ref[...]), cells)
    total = mm_tn(hot, gradients(same))
    faces = bound_ref.shape[1]
    first_row = planes_ref.shape[1] - faces
    for k, step, edge in ((0, -1, slab == 0), (1, 1, slab == slabs - 1)):
        face_row = bound_ref[k : k + 1, :]
        direct = gradients(block_of(lax.rem(slab + step + slabs, slabs)))
        direct = jnp.where(edge, jnp.zeros_like(direct), direct)
        total = total + mm_tn(onehot_rows(face_column(face_row, pick_ref[k]), cells), direct)
        far = jnp.clip(plane + step, 0, planes - 1)
        passed = planes_ref[far, first_row:, :]
        passed = jnp.where(edge & (far != plane), passed, jnp.zeros_like(passed))
        total = total + mm_tn(onehot_rows(column_of(face_row), cells), passed)
    d_out_ref[...] = d_node_ref[...] + total
    partners = same[:, 8:24, :].reshape(16 * peers, feature).astype(BF16)
    coarse = coarse_ref.shape[0]
    cell_row = iota((cells, coarse), 0)
    near = onehot((first_ref[...] == cell_row) | (second_ref[...] == cell_row))
    far = onehot(second_ref[...] - cells == iota((16 * peers, coarse), 0))
    coarse_ref[...] = (0.5 * (mm_tn(near, fresh_ref[...]) + mm_tn(far, partners))).astype(BF16)


def call(kernel, out_shape, *args, scratch=(), smem=(), hbm=(), hbm_out=(), held=(), name=None, cost=None, mib=8):
    def space(i, far):
        return pltpu.HBM if i in far else pltpu.VMEM

    one = not isinstance(out_shape, tuple)
    outs = [pl.BlockSpec(memory_space=space(i, hbm_out)) for i in range(1 if one else len(out_shape))]
    args = [pltpu.with_memory_space_constraint(x, pltpu.HBM) if i in hbm or i in held else x for i, x in enumerate(args)]
    return pl.pallas_call(
        kernel,
        out_shape=out_shape,
        in_specs=[
            pl.BlockSpec(memory_space=pltpu.SMEM if i in smem else space(i, hbm)) for i in range(len(args))
        ],
        out_specs=outs[0] if one else tuple(outs),
        scratch_shapes=list(scratch),
        compiler_params=pltpu.CompilerParams(vmem_limit_bytes=mib * MIB),
        name=name,
        cost_estimate=cost,
    )(*args)


def shape_of(shape, dtype):
    return jax.ShapeDtypeStruct(shape, dtype)


def per_device(
    slabs, node, edges, edge_src, edge_dst, edge_count, intra_idx, bound_idx, cross_pick,
    match_send, pool_first, pool_second, edge_w1, edge_b1, edge_w2, edge_gain,
    node_w1, node_b1, node_w2, node_gain, edge_cot, coarse_cot,
):
    node, edges, edge_cot, coarse_cot = node[0, 0], edges[0, 0], edge_cot[0, 0], coarse_cot[0, 0]
    intra, bound, pick, match = intra_idx[0, 0], bound_idx[0, 0], cross_pick[0], match_send[0, 0]
    first, second = pool_first[0], pool_second[0]
    src, dst = edge_src[0], edge_dst[0]
    cells, feature = node.shape
    slots = edges.shape[0]
    coarse = coarse_cot.shape[0]
    peers = lax.axis_size("sub")
    planes = lax.axis_size("z")
    in_plane = slabs // planes
    dom = ("z", "y1", "y0")
    face = shape_of((8 * peers, feature), BF16)
    wide = -(-(cells + 24 * peers) // 256) * 256

    def swap(rows):
        pairs = [(i - 1, i) for i in range(2, slabs, 2)]
        return lax.ppermute(rows, dom, pairs + [(j, i) for i, j in pairs])

    def exchange(blocks, axes):
        return lax.all_to_all(blocks, axes, split_axis=0, concat_axis=0, tiled=True)

    passed = swap(call(face_kernel, face, node, bound, pick, held=range(3), name="faces"))
    far = (
        node, second, coarse_cot, intra, bound, pick, src, dst, edge_w1, edge_b1[None], edges, edge_w2,
        edge_gain[None], node_w1, node_b1[None], node_w2, node_gain[None], first, match, edge_cot,
    )
    sent, count, onward_pick, *near = call(
        send_kernel,
        (shape_of((2 * peers, FIRST, feature), BF16), shape_of((8, 128), jnp.int32), shape_of((16 * peers, 128), BF16))
        + tuple(shape_of(x.shape, x.dtype) for x in far),
        edge_count, *far,
        smem=(0,), hbm=range(1, 1 + len(far)),
        scratch=[pltpu.SemaphoreType.DMA((len(far),))],
        name="send",
        cost=pl.CostEstimate(flops=60_000_000, bytes_accessed=400_000, transcendentals=0),
    )
    passed = passed.reshape(peers, 8, feature)
    passed = jnp.concatenate([passed, passed], axis=0)
    sent = jnp.concatenate([sent[:, 0:8], passed, sent[:, 16:]], axis=1)
    received = exchange(sent, PAIR)

    new_edges, d_edges, d_node, fresh, sent = call(
        main_kernel,
        (
            shape_of((slots, feature), BF16),
            shape_of((slots, feature), BF16),
            shape_of((cells, feature), F32),
            shape_of((cells, feature), BF16),
            shape_of((in_plane * peers, HEAD + GRAD_ROWS // (in_plane * peers), feature), BF16),
        ),
        count, received, *near[0:3], *near[6:],
        hbm_out=(0, 1),
        scratch=[
            pltpu.VMEM((slots, feature), BF16),
            pltpu.VMEM((slots, feature), BF16),
            pltpu.VMEM((wide, feature), BF16),
            pltpu.VMEM((2 * feature, slots), BF16),
            pltpu.VMEM((wide + cells, slots), BF16),
            pltpu.VMEM((GRAD_ROWS, feature), F32),
            pltpu.SemaphoreType.DMA((2,)),
        ],
        name="layer",
        mib=28,
    )
    received = exchange(sent, PLANE)
    scale = 1.0 / math.sqrt(slabs * peers * slots)

    def total(blocks):
        return jnp.sum(blocks.astype(F32), axis=0)

    def copies(rows, count):
        return jnp.broadcast_to(rows, (count,) + rows.shape)

    ends = jnp.concatenate([received[0:peers, 8:16], received[-peers:, 8:16]], axis=0)
    onward = mm_tn(onward_pick, ends.reshape(16 * peers, feature))[0 : bound.shape[1]]
    rows = jnp.concatenate([total(received[:, HEAD:]), onward], axis=0).astype(BF16)
    by_plane = exchange(copies(rows, planes), "z")
    share = rows.shape[0] - onward.shape[0]
    rows = (total(by_plane[:, 0:share]) * scale).astype(BF16)
    grads = exchange(copies(rows, in_plane * peers), PLANE)
    row = shape_of((1, feature), F32)
    d_node, coarse_out, w1, w2, nw1, nw2, b1, g, nb1, ng = call(
        finish_kernel,
        (
            shape_of((cells, feature), F32),
            shape_of((coarse, feature), BF16),
            shape_of((3 * feature, feature), F32),
            shape_of((feature, feature), F32),
            shape_of((2 * feature, feature), F32),
            shape_of((feature, feature), F32),
            row, row, row, row,
        ),
        received, by_plane, d_node, fresh, *near[3:6], near[17], near[1], grads.reshape(GRAD_ROWS, feature),
        name="finish",
    )
    return (
        new_edges[None, None], coarse_out[None, None], d_node[None, None], d_edges[None, None],
        w1, b1[0], w2, g[0], nw1, nb1[0], nw2, ng[0],
    )


def solution(mesh):
    slabs, peers = mesh.shape["dom"], mesh.shape["sub"]
    devices = mesh.devices.reshape(slabs // 4, 2, 2, peers)
    dom = ("z", "y1", "y0")
    inner = Mesh(devices, dom + ("sub",))
    four, three = P(dom, "sub", None, None), P(dom, "sub", None)
    return jax.shard_map(
        functools.partial(per_device, slabs),
        mesh=inner,
        in_specs=(
            four, four, three, three, P(dom, "sub"), four, four, P("sub", None, None, None),
            four, three, three, P(), P(), P(), P(), P(), P(), P(), P(), four, four,
        ),
        out_specs=(four, four, four, four) + (P(),) * 8,
        check_vma=False,
    )
```
